128 devices in a mesh: passage: 32 (over x, z_hi, y), span: 4 (over z_lo, core).
Axes of the slice: x: 4, y: 4, z: 4 (z_hi: 2, z_lo: 2; z = z_hi * 2 + z_lo), core: 2. Of those that a mesh axis runs over, the one named last changes fastest.
Arguments:
- adjoint: float32 [5, 32, 128, 1024], P(None, 'span', 'passage'), may hold values from -6 to 6
- forcing: float32 [5, 32, 128, 1024], P(None, 'span', 'passage'), may hold values from -6 to 6
- area_scale: float32 [1, 32, 128, 1024], P(None, 'span', 'passage'), may hold values from 0.5 to 2
- azimuth_coupling: float32 [5, 5], replicated, may hold values from -2 to 2
- axial_coupling: float32 [5, 5], replicated, may hold values from -2 to 2
- inverse: float32 [8, 160, 160], P('span'), as said below
- owner_device: int32 [4, 128, 8, 1], P('span', 'passage'), may hold values from 0 to 31; in each aligned block of 32 rows (0 to 31, 32 to 63, ..., all dimensions but the last counted through in order) at most 2 rows name the same one
- owner_slot: int32 [4, 128, 8, 1], P('span', 'passage'), may hold values from 0 to 3
- weight: float32 [4, 128, 8, 1], P('span', 'passage'), may hold values from 0.5 to 1.5
Outputs:
- adjoint_out: float32 [5, 32, 128, 1024], P(None, 'span', 'passage')
The draws below stay inside these ranges and needn't reach their ends.
Inputs may be any that keep to these rules, and one draw needn't show every extreme that they name: `owner_device`: within the inlet points of one device (aligned blocks of 32 entries in order), at most 2 name one passage index; some block reaches 2. Each block is the inverse of a nonsingular radial operator; entries are of order one on the diagonal.
All inputs are finite; a program needn't handle non-finite values.
Results may differ from the reference program's by a relative error of at most 0.00012.
Values sent between devices are 32-bit elements; how exact they have to be, the bound alone decides.
A program may use at most 64 MiB of HBM per device.

```python
import math
import jax
import jax.numpy as jnp
import numpy as np
from jax import lax

NF = 5
R_DEV = 8
A_DEV = 4
NX = 1024
ITERS = 4
NR = 32
NA = 128
XB = 8
CAP = 2
N_PASSAGE = 32
N_SPAN = 4


def draw_inverse(key, part):
    key = jax.random.fold_in(key, 11)
    first, second = jax.random.split(key)
    order = NF * NR
    spread = 0.5 / order ** 0.5
    offdiag = jnp.clip(jax.random.normal(first, (XB, order, order), jnp.float32) * spread, -4.0 * spread, 4.0 * spread)
    diagonal = 1.0 + jax.random.uniform(second, (XB, order, 1), jnp.float32, 0.0, 0.5)
    identity = jnp.eye(order, dtype=jnp.float32)
    return offdiag * (1.0 - identity) + identity * diagonal


def plant(array, stream_key, low, high):
    longest = array.shape.index(max(array.shape))
    spots = []
    for shift in (0, 1):
        where = [jax.random.randint(jax.random.fold_in(stream_key, axis), (), 0, length) for axis, length in enumerate(array.shape)]
        where[longest] = (where[longest] + shift) % array.shape[longest]
        spots.append(tuple(where))
    return array.at[spots[0]].set(low).at[spots[1]].set(high)


def steps_of(stream_key, dims, shards, least, top_value):
    loudness = 1.0
    for axis_at, parts in shards:
        heights = jax.random.uniform(jax.random.fold_in(jax.random.fold_in(stream_key, 6), axis_at), (parts,), jnp.float32, least / len(shards), top_value / len(shards))
        loudness = loudness * jnp.repeat(jnp.exp(heights), dims[axis_at] // parts).reshape((-1,) + (1,) * (len(dims) - 1 - axis_at))
    return loudness


def routed_block(key, own, number, rows, number_of, top, limit, lean):
    order = jax.random.permutation(key, number_of)
    crowded, common = load_shares(number_of, rows * top, limit, lean, True), load_shares(number_of, rows * top, limit, lean, False)
    places = jnp.arange(number_of)

    def named(lengths, rotation):
        used = int((lengths > 0).sum())
        fixed = max(1, used // 4)
        moved = fixed + (places - fixed + rotation * (used - fixed)) % max(1, number_of - fixed)
        return jnp.zeros((number_of,), jnp.int32).at[order[jnp.where(places < fixed, places, moved)]].set(jnp.asarray(lengths, jnp.int32))

    lengths = jnp.where(number % 4 == 0, named(crowded, number // 4), named(common, number - number // 4 - 1))
    mixed = jax.random.permutation(jax.random.fold_in(own, 3), number_of)
    giver, sink = mixed[0:number_of // 2 * 2:2], mixed[1:number_of // 2 * 2:2]
    margin = jnp.minimum(lengths[giver] - 1, limit - lengths[sink]) // 2
    margin = jnp.where((giver == order[0]) | (sink == order[0]) | (lengths[sink] == 0), 0, jnp.maximum(margin, 0))
    moved = jax.random.randint(jax.random.fold_in(own, 4), (number_of // 2,), 0, 1 << 20) % (margin + 1)
    lengths = lengths.at[giver].add(-moved).at[sink].add(moved)
    items = jnp.searchsorted(jnp.cumsum(lengths), jnp.arange(rows * top), side="right").astype(jnp.int32)
    grid = items.reshape(top, rows).T
    grid = grid[jax.random.permutation(jax.random.fold_in(own, 1), rows)]
    rotation = jax.random.randint(jax.random.fold_in(own, 2), (rows, 1), 0, top)
    return jnp.take_along_axis(grid, (jnp.arange(top)[None, :] + rotation) % top, axis=1)


def load_shares(number_of, total, most, lean, full):
    weights = [(1 << 20) // math.isqrt(standing ** lean) + 1 for standing in range(1, number_of + 1)]
    largest = most if full else min(most, max(-(-total // number_of), total * weights[0] // sum(weights)))
    least = 1 if total - largest >= number_of - 1 else 0
    holding, surplus = [largest] + [least] * (number_of - 1), total - largest - least * (number_of - 1)
    while surplus > 0:
        free = [i for i in range(1, number_of) if holding[i] < largest] or [i for i in range(1, number_of) if holding[i] < most]
        pool, remaining = sum([weights[i] for i in free]), surplus
        for i in free:
            more = min(most - holding[i], max(1, remaining * weights[i] // pool), surplus)
            holding[i] = holding[i] + more
            surplus = surplus - more
    return np.array(holding)


def normal_values(key, dims, deviation, bound, cuts=(), held_as=jnp.bfloat16):
    factor_of = steps_of(key, dims, cuts, -0.22, 0.18) if cuts else 1.0
    array = jax.random.normal(key, dims, jnp.float32) * deviation * factor_of
    return jnp.minimum(jnp.maximum(array, -bound), bound).astype(held_as)


def setup_inputs(seed: int = 0) -> dict:
    arg_keys = jax.random.split(jax.random.key(seed), 10)
    adjoint = normal_values(arg_keys[0], (NF, NR, NA, NX), 1.0, 6.0, ((1, 4), (2, 32)), jnp.float32)
    forcing = normal_values(arg_keys[1], (NF, NR, NA, NX), 1.0, 6.0, ((1, 4), (2, 32)), jnp.float32)
    area_scale = jnp.clip(jnp.exp(math.log(2.0) - 1.3862944 * jax.random.uniform(arg_keys[2], (1, NR, NA, NX), jnp.float32) ** steps_of(arg_keys[2], (1, NR, NA, NX), ((1, 4), (2, 32)), -0.2, 0.2)), 0.5, 2.0)
    azimuth_coupling = normal_values(arg_keys[3], (NF, NF), 0.15, 2.0, (), jnp.float32)
    axial_coupling = normal_values(arg_keys[4], (NF, NF), 0.15, 2.0, (), jnp.float32)
    inverse = draw_inverse(jax.random.fold_in(arg_keys[9], 71), 0)
    owner_device_keys = jax.random.split(jax.random.fold_in(arg_keys[6], 1), N_SPAN * NA * R_DEV // (A_DEV * R_DEV))
    owner_device_turns = jax.random.permutation(jax.random.fold_in(arg_keys[6], 3), N_SPAN * NA * R_DEV // (A_DEV * R_DEV))
    owner_device = jax.vmap(lambda own, number: routed_block(jax.random.fold_in(arg_keys[6], 2), own, number, A_DEV * R_DEV, N_PASSAGE, 1, CAP, 2))(owner_device_keys, owner_device_turns).reshape((N_SPAN, NA, R_DEV, 1))
    owner_slot = plant(jax.random.randint(arg_keys[7], (N_SPAN, NA, R_DEV, 1), 0, A_DEV), jax.random.fold_in(arg_keys[7], 1), 0, A_DEV - 1).astype(jnp.int32)
    weight = jnp.clip(0.5 + 1.0 * jax.random.uniform(arg_keys[8], (N_SPAN, NA, R_DEV, 1), jnp.float32) ** steps_of(arg_keys[8], (N_SPAN, NA, R_DEV, 1), ((0, 4), (1, 32)), -0.2, 0.2), 0.5, 1.5)
    return {"adjoint": adjoint, "forcing": forcing, "area_scale": area_scale, "azimuth_coupling": azimuth_coupling, "axial_coupling": axial_coupling, "inverse": inverse, "owner_device": owner_device, "owner_slot": owner_slot, "weight": weight}


HIGHEST_PRECISION = lax.Precision.HIGHEST


def transport(current, extended, axial_ext, area_scale, forcing, azimuth_coupling, axial_coupling):
    azimuth_slope = (-extended[:, :, 4:] + 8.0 * extended[:, :, 3:-1] - 8.0 * extended[:, :, 1:-3] + extended[:, :, :-4]) / 12.0
    axial_slope = (axial_ext[:, :, :, 2:] - axial_ext[:, :, :, :-2]) / 2.0
    coupled = jnp.einsum('fg,grax->frax', azimuth_coupling, azimuth_slope, precision=HIGHEST_PRECISION)
    coupled = coupled + jnp.einsum('fg,grax->frax', axial_coupling, axial_slope, precision=HIGHEST_PRECISION)
    return current - area_scale * coupled + forcing


def radial_solve(right_side, inverse):
    field_count, radial_total, azimuth_total, axial_cells = right_side.shape
    block_count = inverse.shape[0]
    block_width = axial_cells // block_count
    stacked = right_side.reshape(field_count * radial_total, azimuth_total, axial_cells)
    pieces = []
    for block_index in range(block_count):
        piece = stacked[:, :, block_index * block_width:(block_index + 1) * block_width]
        pieces.append(jnp.einsum('ij,jax->iax', inverse[block_index], piece, precision=HIGHEST_PRECISION))
    solved = jnp.concatenate(pieces, axis=2)
    return solved.reshape(field_count, radial_total, azimuth_total, axial_cells)


def reference(adjoint, forcing, area_scale, azimuth_coupling, axial_coupling, inverse, owner_device, owner_slot, weight):
    field_count, radial_total, azimuth_total, axial_cells = adjoint.shape
    owners = owner_device[:, :, :, 0].transpose(0, 2, 1).reshape(radial_total, azimuth_total)
    slots = owner_slot[:, :, :, 0].transpose(0, 2, 1).reshape(radial_total, azimuth_total)
    weights = weight[:, :, :, 0].transpose(0, 2, 1).reshape(radial_total, azimuth_total)
    columns = (owners * A_DEV + slots).astype(jnp.int32)
    targets = jnp.arange(azimuth_total, dtype=jnp.int32)
    interpolate = jnp.where(columns[:, :, None] == targets[None, None, :], weights[:, :, None], jnp.zeros((), weights.dtype))
    current = adjoint
    for sweep_index in range(ITERS):
        extended = jnp.concatenate([current[:, :, -2:], current, current[:, :, :2]], axis=2)
        axial_ext = jnp.pad(current, ((0, 0), (0, 0), (0, 0), (1, 1)))
        exit_plane = jnp.einsum('fra,rab->frb', current[:, :, :, 0], interpolate, precision=HIGHEST_PRECISION)
        right_side = transport(current, extended, axial_ext, area_scale, forcing, azimuth_coupling, axial_coupling)
        right_side = right_side.at[:, :, :, axial_cells - 1].add(exit_plane)
        current = radial_solve(right_side, inverse)
    return current
```

```python
import jax
import jax.numpy as jnp
from jax import lax
from jax.experimental import pallas as pl
from jax.experimental.pallas import tpu as pltpu
from jax.sharding import PartitionSpec as P

ITERS = 4
MESH = pl.DeviceIdType.MESH
NF = 5
R = 8
NR = 32
ROWS = NF * NR
A = 4
CH = 32
TILES = 8
PLANES = 4
FOLD = 40
F32 = jnp.float32
BF16 = jnp.bfloat16


def lanes(shape):
    return lax.broadcasted_iota(jnp.int32, shape, len(shape) - 1)


def roll(x, by):
    by = by % 128
    return x if by == 0 else pltpu.roll(x, by, x.ndim - 1)


def swap_groups(v, lane):
    half = lane < 64
    odd = (lane // 32) % 2 == 1
    c0 = jnp.where(half, v[0], roll(v[2], 64))
    c2 = jnp.where(half, roll(v[0], 64), v[2])
    c1 = jnp.where(half, v[1], roll(v[3], 64))
    c3 = jnp.where(half, roll(v[1], 64), v[3])
    return [
        jnp.where(odd, roll(c1, 32), c0),
        jnp.where(odd, c1, roll(c0, 96)),
        jnp.where(odd, roll(c3, 32), c2),
        jnp.where(odd, c3, roll(c2, 96)),
    ]


def split(x):
    high = x.astype(BF16)
    return high, (x - high.astype(F32)).astype(BF16)


def kernel(
    adj, frc, area, azc, axc, inv, tsend, out,
    sbuf, ext, fa, psend, hal, inl, obuf, tab, tpl, tall, mtab, lhs, rhs, exitb,
    a_send, a_recv, f_send, f_recv, o_send, o_recv,
    az_send, az_recv, ax_send, ax_recv, ex_send, ex_recv,
    t_send, t_recv, u_send, u_recv,
):
    p = lax.axis_index("passage")
    s = lax.axis_index("span")
    plane = p // TILES
    k = p % TILES
    c = s * TILES + k
    first = c == 0
    last = c == CH - 1

    def device(plane_at, chunk):
        return (plane_at * TILES + chunk % TILES, chunk // TILES)

    def remote(src, dst, send, recv, to):
        return pltpu.make_async_remote_copy(
            src_ref=src, dst_ref=dst, send_sem=send, recv_sem=recv,
            device_id=to, device_id_type=MESH,
        )

    def own_rows(span):
        return pl.ds(pl.multiple_of(span * R, R), R)

    barrier = pltpu.get_barrier_semaphore()

    def greet(plane_at, chunk):
        pl.semaphore_signal(barrier, inc=1, device_id=device(plane_at, chunk), device_id_type=MESH)

    def greet_group(t, carry):
        greet(plane, (c + t) % CH)
        return carry

    lax.fori_loop(1, CH, greet_group, 0)
    for d in range(1, PLANES):
        greet((plane + d) % PLANES, c)

    @pl.when(first)
    def _():
        for d in range(1, PLANES):
            greet((plane + d) % PLANES, CH - 1)

    @pl.when(last)
    def _():
        for d in range(1, PLANES):
            greet((plane + d) % PLANES, 0)

    lane8 = lanes((R, 128))

    def regroup(src, field, slot):
        def body(t, carry):
            at = pl.ds(pl.multiple_of(t * 128, 128), 128)
            pieces = swap_groups([src[field, :, j, at] for j in range(A)], lane8)
            for i in range(A):
                sbuf[t * A + i, slot] = pieces[i]
            return carry

        lax.fori_loop(0, CH // A, body, 0)

    for f in range(NF):
        regroup(adj, f, f)
    hal[...] = jnp.zeros_like(hal)

    edge = jnp.logical_or(first, last)
    peers = CH - 1 + PLANES - 1

    @pl.when(edge)
    def _():
        pl.semaphore_wait(barrier, peers + PLANES - 1)

    @pl.when(jnp.logical_not(edge))
    def _():
        pl.semaphore_wait(barrier, peers)

    def adj_copy(to, source):
        return remote(
            sbuf.at[to, pl.ds(0, NF)],
            ext.at[0, 1 + source % TILES, :, own_rows(source // TILES), :],
            a_send.at[to], a_recv.at[source], device(plane, to),
        )

    def frc_copy(to, source):
        return remote(
            sbuf.at[to, pl.ds(NF, NF + 1)],
            fa.at[source % TILES, :, own_rows(source // TILES), :],
            f_send.at[to], f_recv.at[source], device(plane, to),
        )

    def out_copy(to, source):
        return remote(
            ext.at[ITERS, 1 + to % TILES, :, own_rows(to // TILES), :],
            obuf.at[source],
            o_send.at[to], o_recv.at[source], device(plane, to),
        )

    def over_group(do):
        def body(t, carry):
            do((c + t) % CH)
            return carry

        lax.fori_loop(1, CH, body, 0)

    over_group(lambda to: adj_copy(to, c).start())

    table_copy = remote(
        tsend, tab.at[k, own_rows(s), :], t_send, t_recv.at[c], device(plane, CH - 1)
    )

    @pl.when(jnp.logical_not(last))
    def _():
        table_copy.start()

    for f in range(NF):
        regroup(frc, f, NF + f)
    regroup(area, 0, 2 * NF)
    over_group(lambda to: frc_copy(to, c).start())

    ext[0, 1 + k, :, own_rows(s), :] = sbuf[c, 0:NF]
    fa[k, :, own_rows(s), :] = sbuf[c, NF:2 * NF + 1]

    high, low = split(inv[k // (TILES // 2)])
    lhs[0] = high
    lhs[1] = low

    xx32 = lanes((NR, 128)) % 32
    lane160 = lanes((ROWS, 128))
    xx160 = lane160 % 32
    lane40 = lanes((FOLD, 128))
    xx40 = lane40 % 32

    def plane_table(plane_to):
        return remote(
            tpl, tall.at[plane], u_send.at[plane_to], u_recv.at[plane],
            device(plane_to, CH - 1),
        )

    def plane_table_in(plane_from):
        return remote(
            tpl, tall.at[plane_from], u_send.at[plane_from], u_recv.at[plane_from],
            device(plane_from, CH - 1),
        )

    @pl.when(last)
    def _():
        tab[k, own_rows(s), :] = tsend[...]

        def arrived(source, carry):
            remote(
                tsend, tab.at[source % TILES, own_rows(source // TILES), :],
                t_send, t_recv.at[source], device(plane, 0),
            ).wait_recv()
            return carry

        lax.fori_loop(0, CH - 1, arrived, 0)
        merged = jnp.zeros((NR, 128), F32)
        for i in range(TILES):
            merged = jnp.where((xx32 == i) | (xx32 == 16 + i), tab[i], merged)
        tpl[...] = merged
        for d in range(1, PLANES):
            plane_table((plane + d) % PLANES).start()
        tall[plane] = merged
        for d in range(1, PLANES):
            plane_table_in((plane + d) % PLANES).wait_recv()
        column = jnp.zeros((NR, 128), F32)
        weight = jnp.zeros((NR, 128), F32)
        for i in range(PLANES):
            mine = xx32 // 8 == i
            column = jnp.where(mine, roll(tall[i], 8 * i), column)
            weight = jnp.where(mine, roll(tall[i], 8 * i - 16), weight)
        column = column.astype(jnp.int32) - plane * 32

        def masked(b, carry):
            mtab[b] = jnp.where(column == b, weight, 0.0)
            return carry

        lax.fori_loop(0, 32, masked, 0)
        for d in range(1, PLANES):
            plane_table((plane + d) % PLANES).wait_send()

    up = (plane + 1) % PLANES
    down = (plane + PLANES - 1) % PLANES
    nxt = (c + 1) % CH
    prv = (c + CH - 1) % CH

    def az_copy(n, side):
        if side == 0:
            return remote(ext.at[n, 1], ext.at[n, TILES + 1], az_send.at[n, 0], az_recv.at[n, 0], device(down, c))
        return remote(ext.at[n, TILES], ext.at[n, 0], az_send.at[n, 1], az_recv.at[n, 1], device(up, c))

    def ax_copy(n, side):
        if side == 0:
            return remote(psend.at[n, 0], hal.at[n, 1], ax_send.at[n, 0], ax_recv.at[n, 1], device(plane, prv))
        return remote(psend.at[n, 1], hal.at[n, 0], ax_send.at[n, 1], ax_recv.at[n, 0], device(plane, nxt))

    def ax_wait(n, side):
        return remote(psend.at[n, side], hal.at[n, side], ax_send.at[n, side], ax_recv.at[n, side], device(plane, nxt))

    def ex_copy(n, to):
        return remote(psend.at[n, 0], inl.at[n, plane], ex_send.at[n, to], ex_recv.at[n, plane], device(to, CH - 1))

    def ex_wait(n, source):
        return remote(psend.at[n, 0], inl.at[n, source], ex_send.at[n, source], ex_recv.at[n, source], device(source, 0))

    def send_az(n):
        for side in range(2):
            az_copy(n, side).start()

    def send_ax(n):
        edges = [jnp.zeros((FOLD, 128), F32), jnp.zeros((FOLD, 128), F32)]
        for kk in range(TILES):
            tile = ext[n, 1 + kk].reshape(ROWS, 128)
            for g in range(4):
                rows = tile[g * FOLD:(g + 1) * FOLD]
                to = 8 * g + kk
                edges[0] = jnp.where(xx40 == to, roll(rows, to), edges[0])
                edges[1] = jnp.where(xx40 == to, roll(rows, to - 31), edges[1])
        psend[n, 0] = edges[0]
        psend[n, 1] = edges[1]

        @pl.when(jnp.logical_not(first))
        def _():
            ax_copy(n, 0).start()

        @pl.when(jnp.logical_not(last))
        def _():
            ax_copy(n, 1).start()

        @pl.when(first)
        def _():
            for to in range(PLANES):
                ex_copy(n, to).start()

    def wait_adj(source):
        adj_copy(source, source).wait_recv()

    def wait_frc(source):
        frc_copy(source, source).wait_recv()

    over_group(wait_adj)
    send_az(0)
    send_ax(0)
    over_group(wait_frc)

    az = [[azc[f, g] * (1.0 / 12.0) for g in range(NF)] for f in range(NF)]
    ax = [[axc[f, g] * 0.5 for g in range(NF)] for f in range(NF)]

    def couple(coefficients, slope, f):
        total = coefficients[f][0] * slope[0:NR]
        for g in range(1, NF):
            total = total + coefficients[f][g] * slope[g * NR:(g + 1) * NR]
        return total

    def azimuth_part(n, kk):
        here = ext[n, 1 + kk].reshape(ROWS, 128)
        before = ext[n, kk].reshape(ROWS, 128)
        after = ext[n, 2 + kk].reshape(ROWS, 128)
        plus = roll(jnp.where(lane160 >= 32, here, after), 96)
        minus = roll(jnp.where(lane160 < 96, here, before), 32)
        far = roll(
            jnp.where(lane160 >= 64, here, after) - jnp.where(lane160 < 64, here, before), 64
        )
        slope = 8.0 * (plus - minus) - far
        at = slice(kk * 128, (kk + 1) * 128)
        for f in range(NF):
            rows = slice(f * NR, (f + 1) * NR)
            rhs[rows, at] = here[rows] + fa[kk, f] - fa[kk, NF] * couple(az, slope, f)

    def axial_part(n, kk, before, after):
        here = ext[n, 1 + kk].reshape(ROWS, 128)
        slope = jnp.where(xx160 == 31, roll(after, 31 - kk), roll(here, 127)) - jnp.where(
            xx160 == 0, roll(before, -kk), roll(here, 1)
        )
        at = slice(kk * 128, (kk + 1) * 128)
        for f in range(NF):
            rows = slice(f * NR, (f + 1) * NR)
            rhs[rows, at] = rhs[rows, at] - fa[kk, NF] * couple(ax, slope, f)

    def unfold(edge):
        return jnp.concatenate([roll(edge, -8 * g) for g in range(4)], axis=0)

    def exit_plane(n):
        for source in range(PLANES):
            ex_wait(n, source).wait_recv()
        groups = []
        for g in range(4):
            group = jnp.zeros((FOLD, 128), F32)
            for i in range(PLANES):
                group = jnp.where(xx40 // 8 == i, roll(inl[n, i], 8 * (i - g)), group)
            groups.append(group)
        inlet = jnp.concatenate(groups, axis=0)
        exitb[...] = jnp.zeros_like(exitb)
        column = lanes((256, 128))

        def one(b, carry):
            weighted = inlet * jnp.concatenate([mtab[b]] * NF, axis=0)
            pair = jnp.concatenate(split(weighted), axis=1)
            place = (b % A) * 32 + b // A
            ones = (column == place).astype(F32).astype(BF16)
            exitb[...] += jnp.dot(pair, ones, preferred_element_type=F32)
            return carry

        lax.fori_loop(0, 32, one, 0)
        arrived = exitb[...]
        for kk in range(TILES):
            at = slice(kk * 128, (kk + 1) * 128)
            rhs[:, at] = rhs[:, at] + jnp.where(xx160 == 31, roll(arrived, 31 - kk), 0.0)

    def solve(n, pair):
        high, low = split(rhs[:, pair * 256:(pair + 1) * 256])
        solved = jnp.dot(lhs[0], low, preferred_element_type=F32)
        solved = solved + jnp.dot(lhs[1], high, preferred_element_type=F32)
        solved = solved + jnp.dot(lhs[0], high, preferred_element_type=F32)
        for i in range(2):
            ext[n + 1, 1 + 2 * pair + i] = solved[:, i * 128:(i + 1) * 128].reshape(NF, NR, 128)

    def sweep(n, carry):
        for kk in range(1, TILES - 1):
            azimuth_part(n, kk)
        for side in range(2):
            az_copy(n, side).wait_recv()
        azimuth_part(n, 0)
        azimuth_part(n, TILES - 1)

        @pl.when(jnp.logical_not(first))
        def _():
            ax_wait(n, 0).wait_recv()

        @pl.when(jnp.logical_not(last))
        def _():
            ax_wait(n, 1).wait_recv()

        before = unfold(hal[n, 0])
        after = unfold(hal[n, 1])
        for kk in range(TILES):
            axial_part(n, kk, before, after)

        @pl.when(last)
        def _():
            exit_plane(n)

        solve(n, 0)
        solve(n, 3)

        @pl.when(n < ITERS - 1)
        def _():
            send_az(n + 1)

        solve(n, 1)
        solve(n, 2)

        @pl.when(n < ITERS - 1)
        def _():
            send_ax(n + 1)

        return carry

    lax.fori_loop(0, ITERS, sweep, 0)

    over_group(lambda to: out_copy(to, c).start())
    obuf[c] = ext[ITERS, 1 + k, :, own_rows(s), :]
    over_group(lambda source: out_copy(source, source).wait_recv())

    def back(t, carry):
        at = pl.ds(pl.multiple_of(t * 128, 128), 128)
        for f in range(NF):
            pieces = swap_groups([obuf[t * A + i, f] for i in range(A)], lane8)
            for j in range(A):
                out[f, :, j, at] = pieces[j]
        return carry

    lax.fori_loop(0, CH // A, back, 0)

    def sent(to):
        adj_copy(to, c).wait_send()
        frc_copy(to, c).wait_send()
        out_copy(to, c).wait_send()

    over_group(sent)

    @pl.when(jnp.logical_not(last))
    def _():
        table_copy.wait_send()

    def sweep_sent(n, carry):
        for side in range(2):
            az_copy(n, side).wait_send()

        @pl.when(jnp.logical_not(first))
        def _():
            ax_copy(n, 0).wait_send()

        @pl.when(jnp.logical_not(last))
        def _():
            ax_copy(n, 1).wait_send()

        @pl.when(first)
        def _():
            for to in range(PLANES):
                ex_copy(n, to).wait_send()

        return carry

    lax.fori_loop(0, ITERS, sweep_sent, 0)


def table_tile(owner_device, owner_slot, weight):
    column = (owner_device * A + owner_slot).astype(F32).reshape(A, R).T[:, :, None]
    weights = weight.reshape(A, R).T[:, :, None]
    low = jnp.arange(32)[None, None, :] < 16
    return jnp.where(low, column, weights).reshape(R, A * 32)


def per_device(
    adjoint, forcing, area_scale, azimuth_coupling, axial_coupling,
    inverse, owner_device, owner_slot, weight,
):
    vmem = pl.BlockSpec(memory_space=pltpu.VMEM)
    smem = pl.BlockSpec(memory_space=pltpu.SMEM)
    dma = pltpu.SemaphoreType.DMA
    return pl.pallas_call(
        kernel,
        out_shape=jax.ShapeDtypeStruct(adjoint.shape, F32),
        in_specs=[vmem, vmem, vmem, smem, smem, vmem, vmem],
        out_specs=vmem,
        scratch_shapes=[
            pltpu.VMEM((CH, 2 * NF + 1, R, 128), F32),
            pltpu.VMEM((ITERS + 1, TILES + 2, NF, NR, 128), F32),
            pltpu.VMEM((TILES, NF + 1, NR, 128), F32),
            pltpu.VMEM((ITERS, 2, FOLD, 128), F32),
            pltpu.VMEM((ITERS, 2, FOLD, 128), F32),
            pltpu.VMEM((ITERS, PLANES, FOLD, 128), F32),
            pltpu.VMEM((CH, NF, R, 128), F32),
            pltpu.VMEM((TILES, NR, 128), F32),
            pltpu.VMEM((NR, 128), F32),
            pltpu.VMEM((PLANES, NR, 128), F32),
            pltpu.VMEM((32, NR, 128), F32),
            pltpu.VMEM((2, ROWS, ROWS), BF16),
            pltpu.VMEM((ROWS, TILES * 128), F32),
            pltpu.VMEM((ROWS, 128), F32),
            dma((CH,)), dma((CH,)), dma((CH,)), dma((CH,)), dma((CH,)), dma((CH,)),
            dma((ITERS, 2)), dma((ITERS, 2)), dma((ITERS, 2)), dma((ITERS, 2)),
            dma((ITERS, PLANES)), dma((ITERS, PLANES)),
            dma(()), dma((CH,)), dma((PLANES,)), dma((PLANES,)),
        ],
        compiler_params=pltpu.CompilerParams(
            collective_id=0, has_side_effects=True, vmem_limit_bytes=48 * 1024 * 1024
        ),
    )(
        adjoint, forcing, area_scale, azimuth_coupling, axial_coupling, inverse,
        table_tile(owner_device, owner_slot, weight),
    )


def solution(mesh):
    return jax.shard_map(
        per_device,
        mesh=mesh,
        in_specs=(
            P(None, "span", "passage", None),
            P(None, "span", "passage", None),
            P(None, "span", "passage", None),
            P(),
            P(),
            P("span", None, None),
            P("span", "passage", None, None),
            P("span", "passage", None, None),
            P("span", "passage", None, None),
        ),
        out_specs=P(None, "span", "passage", None),
        check_vma=False,
    )
```

```python
import jax
import jax.numpy as jnp
from jax import lax
from jax.experimental import pallas as pl
from jax.experimental.pallas import tpu as pltpu
from jax.sharding import PartitionSpec as P

ITERS = 4
MESH = pl.DeviceIdType.MESH
NF = 5
R = 8
NR = 32
ROWS = NF * NR
A = 4
CH = 32
TILES = 8
PLANES = 4
FOLD = 40
F32 = jnp.float32
BF16 = jnp.bfloat16


def lanes(shape):
    return lax.broadcasted_iota(jnp.int32, shape, len(shape) - 1)


def roll(x, by):
    by = by % 128
    return x if by == 0 else pltpu.roll(x, by, x.ndim - 1)


def swap_groups(v, lane):
    half = lane < 64
    odd = (lane // 32) % 2 == 1
    c0 = jnp.where(half, v[0], roll(v[2], 64))
    c2 = jnp.where(half, roll(v[0], 64), v[2])
    c1 = jnp.where(half, v[1], roll(v[3], 64))
    c3 = jnp.where(half, roll(v[1], 64), v[3])
    return [
        jnp.where(odd, roll(c1, 32), c0),
        jnp.where(odd, c1, roll(c0, 96)),
        jnp.where(odd, roll(c3, 32), c2),
        jnp.where(odd, c3, roll(c2, 96)),
    ]


def split(x):
    high = x.astype(BF16)
    return high, (x - high.astype(F32)).astype(BF16)


def kernel(
    adj, frc, area, azc_in, axc_in, inv_in, owner, slot_in, weight_in, out,
    xin, in_sem, azc, axc, inv, owner_at, slot_at, weight_at, small_sem, tsend, hsend, hrecv, inletb, sbuf, ext, fa, psend, hal, inl, obuf, tab, tpl, tall, mtab, lhs, rhs, exitb,
    a_send, a_recv, f_send, f_recv, o_send, o_recv,
    az_send, az_recv, ax_send, ax_recv, ex_send, ex_recv,
    t_send, t_recv, u_send, u_recv,
):
    p = lax.axis_index("passage")
    s = lax.axis_index("span")
    plane = p // TILES
    k = p % TILES
    c = s * TILES + k
    first = c == 0
    last = c == CH - 1

    def device(plane_at, chunk):
        return (plane_at * TILES + chunk % TILES, chunk // TILES)

    def remote(src, dst, send, recv, to):
        return pltpu.make_async_remote_copy(
            src_ref=src, dst_ref=dst, send_sem=send, recv_sem=recv,
            device_id=to, device_id_type=MESH,
        )

    def own_rows(span):
        return pl.ds(pl.multiple_of(span * R, R), R)

    def load(j, which):
        src, at, count = ((adj, 0, NF), (frc, NF, NF), (area, 2 * NF, 1))[which]
        return pltpu.make_async_copy(
            src.at[:, :, j, :], xin.at[pl.ds(at, count), j], in_sem.at[which, j]
        )

    small = [
        pltpu.make_async_copy(source, to, small_sem.at[i])
        for i, (source, to) in enumerate((
            (owner, owner_at), (slot_in, slot_at), (weight_in, weight_at),
            (azc_in, azc), (axc_in, axc), (inv_in.at[k // (TILES // 2)], inv),
        ))
    ]
    for j in range(A):
        load(j, 0).start()
    for copy in small:
        copy.start()
    for which in range(1, 3):
        for j in range(A):
            load(j, which).start()

    barrier = pltpu.get_barrier_semaphore()

    def greet(plane_at, chunk):
        pl.semaphore_signal(barrier, inc=1, device_id=device(plane_at, chunk), device_id_type=MESH)

    def greet_group(t, carry):
        greet(plane, (c + t) % CH)
        return carry

    lax.fori_loop(1, CH, greet_group, 0)
    for d in range(1, PLANES):
        greet((plane + d) % PLANES, c)

    @pl.when(first)
    def _():
        for d in range(1, PLANES):
            greet((plane + d) % PLANES, CH - 1)

    @pl.when(last)
    def _():
        for d in range(1, PLANES):
            greet((plane + d) % PLANES, 0)

    lane8 = lanes((R, 128))

    def regroup(low, high):
        def body(t, carry):
            at = pl.ds(pl.multiple_of(t * 128, 128), 128)
            for slot in range(low, high):
                pieces = swap_groups([xin[slot, j, :, at] for j in range(A)], lane8)
                for i in range(A):
                    sbuf[t * A + i, slot] = pieces[i]
            return carry

        lax.fori_loop(0, CH // A, body, 0)

    for copy in small[:3]:
        copy.wait()
    diagonal = lax.broadcasted_iota(jnp.int32, (R, R), 0) == lanes((R, R))
    table = jnp.zeros((R, 128), F32)
    for j in range(A):
        column = (owner_at[j] * A + slot_at[j]).astype(F32)
        for i, row in enumerate((column, weight_at[j])):
            upright = jnp.sum(jnp.where(diagonal, row, 0.0), axis=1, keepdims=True)
            table = jnp.where(lane8 // 16 == 2 * j + i, upright, table)
    tsend[...] = table

    for j in range(A):
        load(j, 0).wait()
    regroup(0, NF)
    hal[...] = jnp.zeros_like(hal)

    edge = jnp.logical_or(first, last)
    peers = CH - 1 + PLANES - 1

    @pl.when(edge)
    def _():
        pl.semaphore_wait(barrier, peers + PLANES - 1)

    @pl.when(jnp.logical_not(edge))
    def _():
        pl.semaphore_wait(barrier, peers)

    def adj_copy(to, source):
        return remote(
            sbuf.at[to, pl.ds(0, NF)],
            ext.at[0, source % TILES, :, own_rows(source // TILES), :],
            a_send.at[to], a_recv.at[source], device(plane, to),
        )

    def frc_copy(to, source):
        return remote(
            sbuf.at[to, pl.ds(NF, NF + 1)],
            fa.at[source % TILES, :, own_rows(source // TILES), :],
            f_send.at[to], f_recv.at[source], device(plane, to),
        )

    def out_copy(to, source):
        return remote(
            ext.at[ITERS, to % TILES, :, own_rows(to // TILES), :],
            obuf.at[source],
            o_send.at[to], o_recv.at[source], device(plane, to),
        )

    def over_group(do):
        def body(t, carry):
            do((c + t) % CH)
            return carry

        lax.fori_loop(1, CH, body, 0)

    over_group(lambda to: adj_copy(to, c).start())

    table_copy = remote(
        tsend, tab.at[k, own_rows(s), :], t_send, t_recv.at[c], device(plane, CH - 1)
    )

    @pl.when(jnp.logical_not(last))
    def _():
        table_copy.start()

    for which in range(1, 3):
        for j in range(A):
            load(j, which).wait()
    regroup(NF, 2 * NF + 1)
    over_group(lambda to: frc_copy(to, c).start())

    ext[0, k, :, own_rows(s), :] = sbuf[c, 0:NF]
    fa[k, :, own_rows(s), :] = sbuf[c, NF:2 * NF + 1]

    for copy in small[3:]:
        copy.wait()
    high, low = split(inv[...])
    lhs[0] = high
    lhs[1] = low

    xx32 = lanes((NR, 128)) % 32
    lane32 = lanes((NR, 128))
    lane160 = lanes((ROWS, 128))
    xx160 = lane160 % 32
    lane40 = lanes((FOLD, 128))
    xx40 = lane40 % 32

    def plane_table(plane_to):
        return remote(
            tpl, tall.at[plane], u_send.at[plane_to], u_recv.at[plane],
            device(plane_to, CH - 1),
        )

    def plane_table_in(plane_from):
        return remote(
            tpl, tall.at[plane_from], u_send.at[plane_from], u_recv.at[plane_from],
            device(plane_from, CH - 1),
        )

    @pl.when(last)
    def _():
        tab[k, own_rows(s), :] = tsend[...]

        def arrived(source, carry):
            remote(
                tsend, tab.at[source % TILES, own_rows(source // TILES), :],
                t_send, t_recv.at[source], device(plane, 0),
            ).wait_recv()
            return carry

        lax.fori_loop(0, CH - 1, arrived, 0)
        merged = jnp.zeros((NR, 128), F32)
        for i in range(TILES):
            merged = jnp.where((xx32 == i) | (xx32 == 16 + i), tab[i], merged)
        tpl[...] = merged
        for d in range(1, PLANES):
            plane_table((plane + d) % PLANES).start()
        tall[plane] = merged
        for d in range(1, PLANES):
            plane_table_in((plane + d) % PLANES).wait_recv()
        column = jnp.zeros((NR, 128), F32)
        weight = jnp.zeros((NR, 128), F32)
        for i in range(PLANES):
            mine = xx32 // 8 == i
            column = jnp.where(mine, roll(tall[i], 8 * i), column)
            weight = jnp.where(mine, roll(tall[i], 8 * i - 16), weight)
        column = column.astype(jnp.int32) - plane * 32

        def masked(b, carry):
            mtab[b] = jnp.where(column == b, weight, 0.0)
            return carry

        lax.fori_loop(0, 32, masked, 0)
        for d in range(1, PLANES):
            plane_table((plane + d) % PLANES).wait_send()

    up = (plane + 1) % PLANES
    down = (plane + PLANES - 1) % PLANES
    nxt = (c + 1) % CH
    prv = (c + CH - 1) % CH

    def az_copy(n, side):
        return remote(
            hsend.at[n, side], hrecv.at[n, side], az_send.at[n, side], az_recv.at[n, side],
            device(up if side else down, c),
        )

    def ax_copy(n, side):
        if side == 0:
            return remote(psend.at[n, 0], hal.at[n, 1], ax_send.at[n, 0], ax_recv.at[n, 1], device(plane, prv))
        return remote(psend.at[n, 1], hal.at[n, 0], ax_send.at[n, 1], ax_recv.at[n, 0], device(plane, nxt))

    def ax_wait(n, side):
        return remote(psend.at[n, side], hal.at[n, side], ax_send.at[n, side], ax_recv.at[n, side], device(plane, nxt))

    def ex_copy(n, to):
        return remote(psend.at[n, 0], inl.at[n, plane], ex_send.at[n, to], ex_recv.at[n, plane], device(to, CH - 1))

    def ex_wait(n, source):
        return remote(psend.at[n, 0], inl.at[n, source], ex_send.at[n, source], ex_recv.at[n, source], device(source, 0))

    half80 = lanes((ROWS // 2, 128)) < 64

    def send_az(n):
        for side in range(2):
            tile = ext[n, side * (TILES - 1)].reshape(ROWS, 128)
            near, far = tile[:ROWS // 2], roll(tile[ROWS // 2:], 64)
            hsend[n, side] = jnp.where(half80, far, near) if side else jnp.where(half80, near, far)
            az_copy(n, side).start()

    def halo(n, side):
        packed = hrecv[n, side]
        return jnp.concatenate([packed, roll(packed, 64)], axis=0)

    def send_ax(n):
        edges = [jnp.zeros((FOLD, 128), F32), jnp.zeros((FOLD, 128), F32)]
        for kk in range(TILES):
            tile = ext[n, kk].reshape(ROWS, 128)
            for g in range(4):
                rows = tile[g * FOLD:(g + 1) * FOLD]
                to = 8 * g + kk
                edges[0] = jnp.where(xx40 == to, roll(rows, to), edges[0])
                edges[1] = jnp.where(xx40 == to, roll(rows, to - 31), edges[1])
        psend[n, 0] = edges[0]
        psend[n, 1] = edges[1]

        @pl.when(jnp.logical_not(first))
        def _():
            ax_copy(n, 0).start()

        @pl.when(jnp.logical_not(last))
        def _():
            ax_copy(n, 1).start()

        @pl.when(first)
        def _():
            for to in range(PLANES):
                ex_copy(n, to).start()

    def wait_adj(source):
        adj_copy(source, source).wait_recv()

    def wait_frc(source):
        frc_copy(source, source).wait_recv()

    over_group(wait_adj)
    send_az(0)
    send_ax(0)
    over_group(wait_frc)

    az = [[azc[f, g] * (1.0 / 12.0) for g in range(NF)] for f in range(NF)]
    ax = [[axc[f, g] * 0.5 for g in range(NF)] for f in range(NF)]

    def couple(coefficients, slope, f):
        total = coefficients[f][0] * slope[0:NR]
        for g in range(1, NF):
            total = total + coefficients[f][g] * slope[g * NR:(g + 1) * NR]
        return total

    def azimuth_part(n, kk):
        here = ext[n, kk].reshape(ROWS, 128)
        before = ext[n, kk - 1].reshape(ROWS, 128) if kk else halo(n, 1)
        after = ext[n, kk + 1].reshape(ROWS, 128) if kk < TILES - 1 else halo(n, 0)
        plus = roll(jnp.where(lane160 >= 32, here, after), 96)
        minus = roll(jnp.where(lane160 < 96, here, before), 32)
        far = roll(
            jnp.where(lane160 >= 64, here, after) - jnp.where(lane160 < 64, here, before), 64
        )
        slope = 8.0 * (plus - minus) - far
        at = slice(kk * 128, (kk + 1) * 128)
        for f in range(NF):
            rows = slice(f * NR, (f + 1) * NR)
            rhs[rows, at] = here[rows] + fa[kk, f] - fa[kk, NF] * couple(az, slope, f)

    def axial_part(n, kk, before, after):
        here = ext[n, kk].reshape(ROWS, 128)
        slope = jnp.where(xx160 == 31, roll(after, 31 - kk), roll(here, 127)) - jnp.where(
            xx160 == 0, roll(before, -kk), roll(here, 1)
        )
        at = slice(kk * 128, (kk + 1) * 128)
        for f in range(NF):
            rows = slice(f * NR, (f + 1) * NR)
            rhs[rows, at] = rhs[rows, at] - fa[kk, NF] * couple(ax, slope, f)

    def unfold(edge):
        return jnp.concatenate([roll(edge, -8 * g) for g in range(4)], axis=0)

    def exit_plane(n):
        for source in range(PLANES):
            ex_wait(n, source).wait_recv()
        groups = []
        for g in range(4):
            group = jnp.zeros((FOLD, 128), F32)
            for i in range(PLANES):
                group = jnp.where(xx40 // 8 == i, roll(inl[n, i], 8 * (i - g)), group)
            groups.append(group)
        inletb[...] = jnp.concatenate(groups, axis=0)

        def one(f, carry):
            rows = pl.ds(pl.multiple_of(f * NR, NR), NR)
            inlet = inletb[rows]

            def summed(b, levels):
                if not levels:
                    return inlet * mtab[b]
                (bit, step), rest = levels[0], levels[1:]
                zero, one_ = summed(b, rest), summed(b + step, rest)
                odd = (lane32 // bit) % 2 == 1
                return jnp.where(odd, one_, zero) + roll(jnp.where(odd, zero, one_), -bit)

            total = summed(0, ((64, 2), (32, 1), (4, 16), (2, 8), (1, 4)))
            total = total + roll(total, -8)
            exitb[rows] = total + roll(total, -16)
            return carry

        lax.fori_loop(0, NF, one, 0)
        arrived = exitb[...]
        for kk in range(TILES):
            at = slice(kk * 128, (kk + 1) * 128)
            rhs[:, at] = rhs[:, at] + jnp.where(xx160 == 31, roll(arrived, 31 - kk), 0.0)

    def solve(n, pair):
        high, low = split(rhs[:, pair * 256:(pair + 1) * 256])
        solved = jnp.dot(lhs[0], low, preferred_element_type=F32)
        solved = solved + jnp.dot(lhs[1], high, preferred_element_type=F32)
        solved = solved + jnp.dot(lhs[0], high, preferred_element_type=F32)
        for i in range(2):
            ext[n + 1, 2 * pair + i] = solved[:, i * 128:(i + 1) * 128].reshape(NF, NR, 128)

    def sweep(n, carry):
        for kk in range(1, TILES - 1):
            azimuth_part(n, kk)
        for side in range(2):
            az_copy(n, side).wait_recv()
        azimuth_part(n, 0)
        azimuth_part(n, TILES - 1)

        @pl.when(jnp.logical_not(first))
        def _():
            ax_wait(n, 0).wait_recv()

        @pl.when(jnp.logical_not(last))
        def _():
            ax_wait(n, 1).wait_recv()

        before = unfold(hal[n, 0])
        after = unfold(hal[n, 1])
        for kk in range(TILES):
            axial_part(n, kk, before, after)

        @pl.when(last)
        def _():
            exit_plane(n)

        solve(n, 0)
        solve(n, 3)

        @pl.when(n < ITERS - 1)
        def _():
            send_az(n + 1)

        solve(n, 1)
        solve(n, 2)

        @pl.when(n < ITERS - 1)
        def _():
            send_ax(n + 1)

        return carry

    lax.fori_loop(0, ITERS, sweep, 0)

    over_group(lambda to: out_copy(to, c).start())
    obuf[c] = ext[ITERS, k, :, own_rows(s), :]

    def back(step, carry):
        t = (c // A + CH // A - step) % (CH // A)
        for i in range(A):
            source = t * A + i

            @pl.when(source != c)
            def _():
                out_copy(source, source).wait_recv()

        at = pl.ds(pl.multiple_of(t * 128, 128), 128)
        for f in range(NF):
            pieces = swap_groups([obuf[t * A + i, f] for i in range(A)], lane8)
            for j in range(A):
                out[f, :, j, at] = pieces[j]
        return carry

    lax.fori_loop(1, CH // A + 1, back, 0)

    def sent(to):
        adj_copy(to, c).wait_send()
        frc_copy(to, c).wait_send()
        out_copy(to, c).wait_send()

    over_group(sent)

    @pl.when(jnp.logical_not(last))
    def _():
        table_copy.wait_send()

    def sweep_sent(n, carry):
        for side in range(2):
            az_copy(n, side).wait_send()

        @pl.when(jnp.logical_not(first))
        def _():
            ax_copy(n, 0).wait_send()

        @pl.when(jnp.logical_not(last))
        def _():
            ax_copy(n, 1).wait_send()

        @pl.when(first)
        def _():
            for to in range(PLANES):
                ex_copy(n, to).wait_send()

        return carry

    lax.fori_loop(0, ITERS, sweep_sent, 0)


def per_device(
    adjoint, forcing, area_scale, azimuth_coupling, axial_coupling,
    inverse, owner_device, owner_slot, weight,
):
    vmem = pl.BlockSpec(memory_space=pltpu.VMEM)
    hbm = pl.BlockSpec(memory_space=pltpu.HBM)
    dma = pltpu.SemaphoreType.DMA
    return pl.pallas_call(
        kernel,
        out_shape=jax.ShapeDtypeStruct(adjoint.shape, F32),
        in_specs=[hbm] * 9,
        out_specs=vmem,
        scratch_shapes=[
            pltpu.VMEM((2 * NF + 1, A, R, CH * 32), F32),
            dma((3, A)),
            pltpu.SMEM((NF, NF), F32),
            pltpu.SMEM((NF, NF), F32),
            pltpu.VMEM((ROWS, ROWS), F32),
            pltpu.VMEM((A, 1, R), jnp.int32),
            pltpu.VMEM((A, 1, R), jnp.int32),
            pltpu.VMEM((A, 1, R), F32),
            dma((6,)),
            pltpu.VMEM((R, 128), F32),
            pltpu.VMEM((ITERS, 2, ROWS // 2, 128), F32),
            pltpu.VMEM((ITERS, 2, ROWS // 2, 128), F32),
            pltpu.VMEM((ROWS, 128), F32),
            pltpu.VMEM((CH, 2 * NF + 1, R, 128), F32),
            pltpu.VMEM((ITERS + 1, TILES, NF, NR, 128), F32),
            pltpu.VMEM((TILES, NF + 1, NR, 128), F32),
            pltpu.VMEM((ITERS, 2, FOLD, 128), F32),
            pltpu.VMEM((ITERS, 2, FOLD, 128), F32),
            pltpu.VMEM((ITERS, PLANES, FOLD, 128), F32),
            pltpu.VMEM((CH, NF, R, 128), F32),
            pltpu.VMEM((TILES, NR, 128), F32),
            pltpu.VMEM((NR, 128), F32),
            pltpu.VMEM((PLANES, NR, 128), F32),
            pltpu.VMEM((32, NR, 128), F32),
            pltpu.VMEM((2, ROWS, ROWS), BF16),
            pltpu.VMEM((ROWS, TILES * 128), F32),
            pltpu.VMEM((ROWS, 128), F32),
            dma((CH,)), dma((CH,)), dma((CH,)), dma((CH,)), dma((CH,)), dma((CH,)),
            dma((ITERS, 2)), dma((ITERS, 2)), dma((ITERS, 2)), dma((ITERS, 2)),
            dma((ITERS, PLANES)), dma((ITERS, PLANES)),
            dma(()), dma((CH,)), dma((PLANES,)), dma((PLANES,)),
        ],
        compiler_params=pltpu.CompilerParams(
            collective_id=0, has_side_effects=True, vmem_limit_bytes=60 * 1024 * 1024
        ),
    )(
        adjoint, forcing, area_scale, azimuth_coupling, axial_coupling, inverse,
        owner_device.reshape(A, 1, R), owner_slot.reshape(A, 1, R), weight.reshape(A, 1, R),
    )


def solution(mesh):
    return jax.shard_map(
        per_device,
        mesh=mesh,
        in_specs=(
            P(None, "span", "passage", None),
            P(None, "span", "passage", None),
            P(None, "span", "passage", None),
            P(),
            P(),
            P("span", None, None),
            P("span", "passage", None, None),
            P("span", "passage", None, None),
            P("span", "passage", None, None),
        ),
        out_specs=P(None, "span", "passage", None),
        check_vma=False,
    )
```

```python
import jax
import jax.numpy as jnp
from jax import lax
from jax.experimental import pallas as pl
from jax.experimental.pallas import tpu as pltpu
from jax.sharding import PartitionSpec as P

ITERS = 4
MESH = pl.DeviceIdType.MESH
NF = 5
R = 8
NR = 32
ROWS = NF * NR
A = 4
CH = 32
TILES = 8
PLANES = 4
FOLD = 40
F32 = jnp.float32
BF16 = jnp.bfloat16


def lanes(shape):
    return lax.broadcasted_iota(jnp.int32, shape, len(shape) - 1)


def roll(x, by):
    by = by % 128
    return x if by == 0 else pltpu.roll(x, by, x.ndim - 1)


def swap_groups(v, lane):
    half = lane < 64
    odd = (lane // 32) % 2 == 1
    c0 = jnp.where(half, v[0], roll(v[2], 64))
    c2 = jnp.where(half, roll(v[0], 64), v[2])
    c1 = jnp.where(half, v[1], roll(v[3], 64))
    c3 = jnp.where(half, roll(v[1], 64), v[3])
    return [
        jnp.where(odd, roll(c1, 32), c0),
        jnp.where(odd, c1, roll(c0, 96)),
        jnp.where(odd, roll(c3, 32), c2),
        jnp.where(odd, c3, roll(c2, 96)),
    ]


def split(x):
    high = x.astype(BF16)
    return high, (x - high.astype(F32)).astype(BF16)


def kernel(
    adj, frc, area, azc_in, axc_in, inv_in, owner, slot_in, weight_in, out,
    xin, in_sem, azc, axc, inv, owner_at, slot_at, weight_at, small_sem, tsend, hsend, hrecv, sbuf, ext, fa, psend, hal, inl, obuf, tab, tpl, tall, mtab, lhs, rhs,
    a_send, a_recv, f_send, f_recv, o_send, o_recv,
    az_send, az_recv, ax_send, ax_recv, ex_send, ex_recv,
    t_send, t_recv, u_send, u_recv,
):
    p = lax.axis_index("passage")
    s = lax.axis_index("span")
    plane = p // TILES
    k = p % TILES
    c = s * TILES + k
    first = c == 0
    last = c == CH - 1

    def device(plane_at, chunk):
        return (plane_at * TILES + chunk % TILES, chunk // TILES)

    def remote(src, dst, send, recv, to):
        return pltpu.make_async_remote_copy(
            src_ref=src, dst_ref=dst, send_sem=send, recv_sem=recv,
            device_id=to, device_id_type=MESH,
        )

    def own_rows(span):
        return pl.ds(pl.multiple_of(span * R, R), R)

    def load(j, which):
        src, at, count = ((adj, 0, NF), (area, NF, 1), (frc, NF + 1, NF))[which]
        return pltpu.make_async_copy(
            src.at[:, :, j, :], xin.at[pl.ds(at, count), j], in_sem.at[which, j]
        )

    small = [
        pltpu.make_async_copy(source, to, small_sem.at[i])
        for i, (source, to) in enumerate((
            (owner, owner_at), (slot_in, slot_at), (weight_in, weight_at),
            (azc_in, azc), (axc_in, axc), (inv_in.at[k // (TILES // 2)], inv),
        ))
    ]
    for j in range(A):
        load(j, 0).start()
    for copy in small:
        copy.start()
    for which in range(1, 3):
        for j in range(A):
            load(j, which).start()

    barrier = pltpu.get_barrier_semaphore()

    def greet(plane_at, chunk):
        pl.semaphore_signal(barrier, inc=1, device_id=device(plane_at, chunk), device_id_type=MESH)

    def greet_group(t, carry):
        greet(plane, (c + t) % CH)
        return carry

    lax.fori_loop(1, CH, greet_group, 0)
    for d in range(1, PLANES):
        greet((plane + d) % PLANES, c)

    @pl.when(first)
    def _():
        for d in range(1, PLANES):
            greet((plane + d) % PLANES, CH - 1)

    @pl.when(last)
    def _():
        for d in range(1, PLANES):
            greet((plane + d) % PLANES, 0)

    lane8 = lanes((R, 128))

    def regroup(low, high):
        def body(t, carry):
            at = pl.ds(pl.multiple_of(t * 128, 128), 128)
            for slot in range(low, high):
                pieces = swap_groups([xin[slot, j, :, at] for j in range(A)], lane8)
                for i in range(A):
                    sbuf[t * A + i, slot] = pieces[i]
            return carry

        lax.fori_loop(0, CH // A, body, 0)

    for copy in small[:3]:
        copy.wait()
    diagonal = lax.broadcasted_iota(jnp.int32, (R, R), 0) == lanes((R, R))
    table = jnp.zeros((R, 128), F32)
    for j in range(A):
        column = (owner_at[j] * A + slot_at[j]).astype(F32)
        for i, row in enumerate((column, weight_at[j])):
            upright = jnp.sum(jnp.where(diagonal, row, 0.0), axis=1, keepdims=True)
            table = jnp.where(lane8 // 16 == 2 * j + i, upright, table)
    tsend[...] = table

    for which in range(2):
        for j in range(A):
            load(j, which).wait()
    regroup(0, NF + 1)
    hal[...] = jnp.zeros_like(hal)

    edge = jnp.logical_or(first, last)
    peers = CH - 1 + PLANES - 1

    @pl.when(edge)
    def _():
        pl.semaphore_wait(barrier, peers + PLANES - 1)

    @pl.when(jnp.logical_not(edge))
    def _():
        pl.semaphore_wait(barrier, peers)

    def adj_copy(to, source):
        return remote(
            sbuf.at[to, pl.ds(0, NF + 1)],
            ext.at[0, source % TILES, :, own_rows(source // TILES), :],
            a_send.at[to], a_recv.at[source], device(plane, to),
        )

    def frc_copy(to, source):
        return remote(
            sbuf.at[to, pl.ds(NF + 1, NF)],
            fa.at[source % TILES, :, own_rows(source // TILES), :],
            f_send.at[to], f_recv.at[source], device(plane, to),
        )

    def out_copy(to, source):
        return remote(
            ext.at[ITERS, to % TILES, pl.ds(0, NF), own_rows(to // TILES), :],
            obuf.at[source],
            o_send.at[to], o_recv.at[source], device(plane, to),
        )

    def over_group(do):
        def body(t, carry):
            do((c + t) % CH)
            return carry

        lax.fori_loop(1, CH, body, 0)

    over_group(lambda to: adj_copy(to, c).start())

    table_copy = remote(
        tsend, tab.at[k, own_rows(s), :], t_send, t_recv.at[c], device(plane, CH - 1)
    )

    @pl.when(jnp.logical_not(last))
    def _():
        table_copy.start()

    for j in range(A):
        load(j, 2).wait()
    regroup(NF + 1, 2 * NF + 1)
    over_group(lambda to: frc_copy(to, c).start())

    ext[0, k, :, own_rows(s), :] = sbuf[c, 0:NF + 1]
    fa[k, :, own_rows(s), :] = sbuf[c, NF + 1:2 * NF + 1]

    for copy in small[3:]:
        copy.wait()
    high, low = split(inv[...])
    lhs[0] = high
    lhs[1] = low

    xx32 = lanes((NR, 128)) % 32
    lane160 = lanes((ROWS, 128))
    xx160 = lane160 % 32
    lane40 = lanes((FOLD, 128))
    xx40 = lane40 % 32

    def plane_table(plane_to):
        return remote(
            tpl, tall.at[plane], u_send.at[plane_to], u_recv.at[plane],
            device(plane_to, CH - 1),
        )

    def plane_table_in(plane_from):
        return remote(
            tpl, tall.at[plane_from], u_send.at[plane_from], u_recv.at[plane_from],
            device(plane_from, CH - 1),
        )

    @pl.when(last)
    def _():
        tab[k, own_rows(s), :] = tsend[...]

        def arrived(source, carry):
            remote(
                tsend, tab.at[source % TILES, own_rows(source // TILES), :],
                t_send, t_recv.at[source], device(plane, 0),
            ).wait_recv()
            return carry

        lax.fori_loop(0, CH - 1, arrived, 0)
        merged = jnp.zeros((NR, 128), F32)
        for i in range(TILES):
            merged = jnp.where((xx32 == i) | (xx32 == 16 + i), tab[i], merged)
        tpl[...] = merged
        for d in range(1, PLANES):
            plane_table((plane + d) % PLANES).start()
        tall[plane] = merged
        for d in range(1, PLANES):
            plane_table_in((plane + d) % PLANES).wait_recv()
        column = jnp.zeros((NR, 128), F32)
        weight = jnp.zeros((NR, 128), F32)
        for i in range(PLANES):
            mine = xx32 // 8 == i
            column = jnp.where(mine, roll(tall[i], 8 * i), column)
            weight = jnp.where(mine, roll(tall[i], 8 * i - 16), weight)
        column = column - (plane * 32).astype(F32)
        here = (4 * (lanes((NR, 128)) % 8)).astype(F32)
        for shift in range(8):
            columns, weights = roll(column, -shift), roll(weight, -shift)
            for j in range(A):
                mtab[j, shift] = jnp.where(columns == here + j, weights, 0.0)
        for d in range(1, PLANES):
            plane_table((plane + d) % PLANES).wait_send()

    up = (plane + 1) % PLANES
    down = (plane + PLANES - 1) % PLANES
    nxt = (c + 1) % CH
    prv = (c + CH - 1) % CH

    def az_copy(n, side):
        return remote(
            hsend.at[n, side], hrecv.at[n, side], az_send.at[n, side], az_recv.at[n, side],
            device(up if side else down, c),
        )

    def ax_copy(n, side):
        if side == 0:
            return remote(psend.at[n, 0], hal.at[n, 1], ax_send.at[n, 0], ax_recv.at[n, 1], device(plane, prv))
        return remote(psend.at[n, 1], hal.at[n, 0], ax_send.at[n, 1], ax_recv.at[n, 0], device(plane, nxt))

    def ax_wait(n, side):
        return remote(psend.at[n, side], hal.at[n, side], ax_send.at[n, side], ax_recv.at[n, side], device(plane, nxt))

    def ex_copy(n, to):
        return remote(psend.at[n, 0], inl.at[n, plane], ex_send.at[n, to], ex_recv.at[n, plane], device(to, CH - 1))

    def ex_wait(n, source):
        return remote(psend.at[n, 0], inl.at[n, source], ex_send.at[n, source], ex_recv.at[n, source], device(source, 0))

    def field(n, kk):
        return ext[n, kk, 0:NF].reshape(ROWS, 128)

    half80 = lanes((ROWS // 2, 128)) < 64

    def send_az(n):
        for side in range(2):
            tile = field(n, side * (TILES - 1))
            near, far = tile[:ROWS // 2], roll(tile[ROWS // 2:], 64)
            hsend[n, side] = jnp.where(half80, far, near) if side else jnp.where(half80, near, far)
            az_copy(n, side).start()

    def halo(n, side):
        packed = hrecv[n, side]
        return jnp.concatenate([packed, roll(packed, 64)], axis=0)

    def send_ax(n):
        edges = [jnp.zeros((FOLD, 128), F32), jnp.zeros((FOLD, 128), F32)]
        for kk in range(TILES):
            tile = field(n, kk).reshape(NF, 4, R, 128)
            for q in range(4):
                rows = tile[:, q].reshape(FOLD, 128)
                to = 8 * q + kk
                edges[0] = jnp.where(xx40 == to, roll(rows, to), edges[0])
                edges[1] = jnp.where(xx40 == to, roll(rows, to - 31), edges[1])
        psend[n, 0] = edges[0]
        psend[n, 1] = edges[1]

        @pl.when(jnp.logical_not(first))
        def _():
            ax_copy(n, 0).start()

        @pl.when(jnp.logical_not(last))
        def _():
            ax_copy(n, 1).start()

        @pl.when(first)
        def _():
            for to in range(PLANES):
                ex_copy(n, to).start()

    def wait_adj(source):
        adj_copy(source, source).wait_recv()

    def wait_frc(source):
        frc_copy(source, source).wait_recv()

    over_group(wait_adj)
    send_az(0)
    send_ax(0)
    az = [[azc[f, g] * (1.0 / 12.0) for g in range(NF)] for f in range(NF)]
    ax = [[axc[f, g] * 0.5 for g in range(NF)] for f in range(NF)]

    def couple(coefficients, slope, f):
        total = coefficients[f][0] * slope[0:NR]
        for g in range(1, NF):
            total = total + coefficients[f][g] * slope[g * NR:(g + 1) * NR]
        return total

    def stencils(n, kk):
        here = field(n, kk)
        before = field(n, kk - 1) if kk else halo(n, 1)
        after = field(n, kk + 1) if kk < TILES - 1 else halo(n, 0)
        plus = roll(jnp.where(lane160 >= 32, here, after), 96)
        minus = roll(jnp.where(lane160 < 96, here, before), 32)
        far = roll(
            jnp.where(lane160 >= 64, here, after) - jnp.where(lane160 < 64, here, before), 64
        )
        slope = 8.0 * (plus - minus) - far
        along = jnp.where(xx160 == 31, 0.0, roll(here, 127)) - jnp.where(
            xx160 == 0, 0.0, roll(here, 1)
        )
        for f in range(NF):
            coupled = couple(az, slope, f) + couple(ax, along, f)
            right = here[f * NR:(f + 1) * NR] - ext[0, kk, NF] * coupled
            rhs[kk, f] = right.reshape(4, R, 128)

    def couple_edges(n):
        sides = []
        for side, sign in ((0, -1.0), (1, 1.0)):
            edge = hal[n, side].reshape(NF, R, 128)
            rows = []
            for f in range(NF):
                total = ax[f][0] * edge[0]
                for g in range(1, NF):
                    total = total + ax[f][g] * edge[g]
                rows.append(sign * total)
            sides.append(jnp.concatenate(rows, axis=0))
        return sides

    def with_edges(kk, edges):
        right = rhs[kk]
        groups = []
        for q in range(4):
            at = 8 * q + kk
            edge = jnp.where(
                xx40 == 31, roll(edges[1], 31 - at), jnp.where(xx40 == 0, roll(edges[0], -at), 0.0)
            ).reshape(NF, R, 128)
            scale = ext[0, kk, NF, q * R:(q + 1) * R]
            groups.append(
                right[:, q] + fa[kk, :, q * R:(q + 1) * R] - scale[None] * edge
            )
        return jnp.stack(groups, axis=1).reshape(ROWS, 128)

    def exit_plane(n):
        for source in range(PLANES):
            ex_wait(n, source).wait_recv()
        for q in range(4):
            inlet = jnp.zeros((FOLD, 128), F32)
            for i in range(PLANES):
                inlet = jnp.where(xx40 // 8 == i, roll(inl[n, i], 8 * (i - q)), inlet)
            sums = [None] * A
            for shift in range(8):
                moved = roll(inlet, -shift)
                for j in range(A):
                    tile = mtab[j, shift, q * R:(q + 1) * R]
                    term = moved * jnp.concatenate([tile] * NF, axis=0)
                    sums[j] = term if sums[j] is None else sums[j] + term
            odd = (lane40 // 32) % 2 == 1
            pairs = [
                jnp.where(odd, sums[j + 1], sums[j]) + roll(jnp.where(odd, sums[j], sums[j + 1]), -32)
                for j in (0, 2)
            ]
            upper = lane40 >= 64
            total = jnp.where(upper, pairs[1], pairs[0]) + roll(
                jnp.where(upper, pairs[0], pairs[1]), -64
            )
            total = total + roll(total, -8)
            total = total + roll(total, -16)
            for kk in range(TILES):
                placed = jnp.where(xx40 == 31, roll(total, 31 - kk), 0.0)
                rhs[kk, :, q] += placed.reshape(NF, R, 128)

    def solve(n, pair, edges):
        high, low = split(jnp.concatenate(
            [with_edges(2 * pair + i, edges) for i in range(2)], axis=1
        ))
        solved = jnp.dot(lhs[0], low, preferred_element_type=F32)
        solved = solved + jnp.dot(lhs[1], high, preferred_element_type=F32)
        solved = solved + jnp.dot(lhs[0], high, preferred_element_type=F32)
        for i in range(2):
            ext[n + 1, 2 * pair + i, 0:NF] = solved[:, i * 128:(i + 1) * 128].reshape(NF, NR, 128)

    def sweep(n, carry):
        for kk in range(1, TILES - 1):
            stencils(n, kk)
        for side in range(2):
            az_copy(n, side).wait_recv()
        stencils(n, 0)
        stencils(n, TILES - 1)

        @pl.when(jnp.logical_not(first))
        def _():
            ax_wait(n, 0).wait_recv()

        @pl.when(jnp.logical_not(last))
        def _():
            ax_wait(n, 1).wait_recv()

        @pl.when(n == 0)
        def _():
            over_group(wait_frc)

        edges = couple_edges(n)

        @pl.when(last)
        def _():
            exit_plane(n)

        solve(n, 0, edges)
        solve(n, 3, edges)

        @pl.when(n < ITERS - 1)
        def _():
            send_az(n + 1)

        solve(n, 1, edges)
        solve(n, 2, edges)

        @pl.when(n < ITERS - 1)
        def _():
            send_ax(n + 1)

        return carry

    lax.fori_loop(0, ITERS, sweep, 0)

    over_group(lambda to: out_copy(to, c).start())
    obuf[c] = ext[ITERS, k, 0:NF, own_rows(s), :]

    def back(step, carry):
        t = (c // A + CH // A - step) % (CH // A)
        for i in range(A):
            source = t * A + i

            @pl.when(source != c)
            def _():
                out_copy(source, source).wait_recv()

        at = pl.ds(pl.multiple_of(t * 128, 128), 128)
        for f in range(NF):
            pieces = swap_groups([obuf[t * A + i, f] for i in range(A)], lane8)
            for j in range(A):
                out[f, :, j, at] = pieces[j]
        return carry

    lax.fori_loop(1, CH // A + 1, back, 0)

    def sent(to):
        adj_copy(to, c).wait_send()
        frc_copy(to, c).wait_send()
        out_copy(to, c).wait_send()

    over_group(sent)

    @pl.when(jnp.logical_not(last))
    def _():
        table_copy.wait_send()

    def sweep_sent(n, carry):
        for side in range(2):
            az_copy(n, side).wait_send()

        @pl.when(jnp.logical_not(first))
        def _():
            ax_copy(n, 0).wait_send()

        @pl.when(jnp.logical_not(last))
        def _():
            ax_copy(n, 1).wait_send()

        @pl.when(first)
        def _():
            for to in range(PLANES):
                ex_copy(n, to).wait_send()

        return carry

    lax.fori_loop(0, ITERS, sweep_sent, 0)


def per_device(
    adjoint, forcing, area_scale, azimuth_coupling, axial_coupling,
    inverse, owner_device, owner_slot, weight,
):
    vmem = pl.BlockSpec(memory_space=pltpu.VMEM)
    hbm = pl.BlockSpec(memory_space=pltpu.HBM)
    dma = pltpu.SemaphoreType.DMA
    return pl.pallas_call(
        kernel,
        out_shape=jax.ShapeDtypeStruct(adjoint.shape, F32),
        in_specs=[hbm] * 9,
        out_specs=vmem,
        scratch_shapes=[
            pltpu.VMEM((2 * NF + 1, A, R, CH * 32), F32),
            dma((3, A)),
            pltpu.SMEM((NF, NF), F32),
            pltpu.SMEM((NF, NF), F32),
            pltpu.VMEM((ROWS, ROWS), F32),
            pltpu.VMEM((A, 1, R), jnp.int32),
            pltpu.VMEM((A, 1, R), jnp.int32),
            pltpu.VMEM((A, 1, R), F32),
            dma((6,)),
            pltpu.VMEM((R, 128), F32),
            pltpu.VMEM((ITERS, 2, ROWS // 2, 128), F32),
            pltpu.VMEM((ITERS, 2, ROWS // 2, 128), F32),
            pltpu.VMEM((CH, 2 * NF + 1, R, 128), F32),
            pltpu.VMEM((ITERS + 1, TILES, NF + 1, NR, 128), F32),
            pltpu.VMEM((TILES, NF, NR, 128), F32),
            pltpu.VMEM((ITERS, 2, FOLD, 128), F32),
            pltpu.VMEM((ITERS, 2, FOLD, 128), F32),
            pltpu.VMEM((ITERS, PLANES, FOLD, 128), F32),
            pltpu.VMEM((CH, NF, R, 128), F32),
            pltpu.VMEM((TILES, NR, 128), F32),
            pltpu.VMEM((NR, 128), F32),
            pltpu.VMEM((PLANES, NR, 128), F32),
            pltpu.VMEM((A, 8, NR, 128), F32),
            pltpu.VMEM((2, ROWS, ROWS), BF16),
            pltpu.VMEM((TILES, NF, 4, R, 128), F32),
            dma((CH,)), dma((CH,)), dma((CH,)), dma((CH,)), dma((CH,)), dma((CH,)),
            dma((ITERS, 2)), dma((ITERS, 2)), dma((ITERS, 2)), dma((ITERS, 2)),
            dma((ITERS, PLANES)), dma((ITERS, PLANES)),
            dma(()), dma((CH,)), dma((PLANES,)), dma((PLANES,)),
        ],
        compiler_params=pltpu.CompilerParams(
            collective_id=0, has_side_effects=True, vmem_limit_bytes=60 * 1024 * 1024
        ),
    )(
        adjoint, forcing, area_scale, azimuth_coupling, axial_coupling, inverse,
        owner_device.reshape(A, 1, R), owner_slot.reshape(A, 1, R), weight.reshape(A, 1, R),
    )


def solution(mesh):
    return jax.shard_map(
        per_device,
        mesh=mesh,
        in_specs=(
            P(None, "span", "passage", None),
            P(None, "span", "passage", None),
            P(None, "span", "passage", None),
            P(),
            P(),
            P("span", None, None),
            P("span", "passage", None, None),
            P("span", "passage", None, None),
            P("span", "passage", None, None),
        ),
        out_specs=P(None, "span", "passage", None),
        check_vma=False,
    )
```

```python
import jax
import jax.numpy as jnp
from jax import lax
from jax.experimental import pallas as pl
from jax.experimental.pallas import tpu as pltpu
from jax.sharding import PartitionSpec as P

ITERS = 4
MESH = pl.DeviceIdType.MESH
NF = 5
R = 8
NR = 32
ROWS = NF * NR
A = 4
CH = 32
TILES = 8
PLANES = 4
FOLD = 40
F32 = jnp.float32
BF16 = jnp.bfloat16


def flip(member):
    span, k = member // TILES, member % TILES
    at = k + k // 4 * (11 - 2 * k)
    return span * TILES + at + span % 2 * (7 - 2 * at)


def unflip(chunk):
    span, at = chunk // TILES, chunk % TILES
    at = at + span % 2 * (7 - 2 * at)
    return span * TILES + at + at // 4 * (11 - 2 * at)


LAST = unflip(CH - 1)


def lanes(shape):
    return lax.broadcasted_iota(jnp.int32, shape, len(shape) - 1)


def roll(x, by):
    by = by % 128
    return x if by == 0 else pltpu.roll(x, by, x.ndim - 1)


def swap_groups(v, lane):
    half = lane < 64
    odd = (lane // 32) % 2 == 1
    c0 = jnp.where(half, v[0], roll(v[2], 64))
    c2 = jnp.where(half, roll(v[0], 64), v[2])
    c1 = jnp.where(half, v[1], roll(v[3], 64))
    c3 = jnp.where(half, roll(v[1], 64), v[3])
    return [
        jnp.where(odd, roll(c1, 32), c0),
        jnp.where(odd, c1, roll(c0, 96)),
        jnp.where(odd, roll(c3, 32), c2),
        jnp.where(odd, c3, roll(c2, 96)),
    ]


def split(x):
    high = x.astype(BF16)
    return high, (x - high.astype(F32)).astype(BF16)


def kernel(
    adj, frc, area, azc_in, axc_in, inv_in, owner, slot_in, weight_in, out,
    xin, in_sem, azc, axc, inv, owner_at, slot_at, weight_at, small_sem, tsend, hsend, hrecv, sbuf, ext, fa, psend, hal, inl, obuf, tab, tpl, tall, mtab, lhs, rhs,
    a_send, a_recv, f_send, f_recv, o_send, o_recv,
    az_send, az_recv, ax_send, ax_recv, ex_send, ex_recv,
    t_send, t_recv, u_send, u_recv,
):
    p = lax.axis_index("passage")
    s = lax.axis_index("span")
    plane = p // TILES
    k = p % TILES
    c = s * TILES + k
    chunk = flip(c)
    first = chunk == 0
    last = chunk == CH - 1

    def device(plane_at, chunk):
        return (plane_at * TILES + chunk % TILES, chunk // TILES)

    def remote(src, dst, send, recv, to):
        return pltpu.make_async_remote_copy(
            src_ref=src, dst_ref=dst, send_sem=send, recv_sem=recv,
            device_id=to, device_id_type=MESH,
        )

    def own_rows(span):
        return pl.ds(pl.multiple_of(span * R, R), R)

    def load(j, which):
        src, at, count = ((adj, 0, NF), (area, NF, 1), (frc, NF + 1, NF))[which]
        return pltpu.make_async_copy(
            src.at[:, :, j, :], xin.at[pl.ds(at, count), j], in_sem.at[which, j]
        )

    small = [
        pltpu.make_async_copy(source, to, small_sem.at[i])
        for i, (source, to) in enumerate((
            (owner, owner_at), (slot_in, slot_at), (weight_in, weight_at),
            (azc_in, azc), (axc_in, axc), (inv_in.at[chunk % TILES // (TILES // 2)], inv),
        ))
    ]
    for j in range(A):
        load(j, 0).start()
    for copy in small:
        copy.start()
    for which in range(1, 3):
        for j in range(A):
            load(j, which).start()

    barrier = pltpu.get_barrier_semaphore()

    def greet(plane_at, chunk):
        pl.semaphore_signal(barrier, inc=1, device_id=device(plane_at, chunk), device_id_type=MESH)

    def greet_group(t, carry):
        greet(plane, (c + t) % CH)
        return carry

    lax.fori_loop(1, CH, greet_group, 0)
    for d in range(1, PLANES):
        greet((plane + d) % PLANES, c)

    @pl.when(first)
    def _():
        for d in range(1, PLANES):
            greet((plane + d) % PLANES, LAST)

    @pl.when(last)
    def _():
        for d in range(1, PLANES):
            greet((plane + d) % PLANES, 0)

    lane8 = lanes((R, 128))

    def regroup(low, high):
        def body(t, carry):
            at = pl.ds(pl.multiple_of(t * 128, 128), 128)
            for slot in range(low, high):
                pieces = swap_groups([xin[slot, j, :, at] for j in range(A)], lane8)
                for i in range(A):
                    sbuf[t * A + i, slot] = pieces[i]
            return carry

        lax.fori_loop(0, CH // A, body, 0)

    for copy in small[:3]:
        copy.wait()
    diagonal = lax.broadcasted_iota(jnp.int32, (R, R), 0) == lanes((R, R))
    table = jnp.zeros((R, 128), F32)
    for j in range(A):
        column = (owner_at[j] * A + slot_at[j]).astype(F32)
        for i, row in enumerate((column, weight_at[j])):
            upright = jnp.sum(jnp.where(diagonal, row, 0.0), axis=1, keepdims=True)
            table = jnp.where(lane8 // 16 == 2 * j + i, upright, table)
    tsend[...] = table

    for which in range(2):
        for j in range(A):
            load(j, which).wait()
    regroup(0, NF + 1)
    hal[...] = jnp.zeros_like(hal)

    edge = jnp.logical_or(first, last)
    peers = CH - 1 + PLANES - 1

    @pl.when(edge)
    def _():
        pl.semaphore_wait(barrier, peers + PLANES - 1)

    @pl.when(jnp.logical_not(edge))
    def _():
        pl.semaphore_wait(barrier, peers)

    def adj_copy(to, source):
        return remote(
            sbuf.at[flip(to), pl.ds(0, NF + 1)],
            ext.at[0, source % TILES, :, own_rows(source // TILES), :],
            a_send.at[to], a_recv.at[source], device(plane, to),
        )

    def frc_copy(to, source):
        return remote(
            sbuf.at[flip(to), pl.ds(NF + 1, NF)],
            fa.at[source % TILES, :, own_rows(source // TILES), :],
            f_send.at[to], f_recv.at[source], device(plane, to),
        )

    def out_copy(to, source):
        return remote(
            ext.at[ITERS, to % TILES, pl.ds(0, NF), own_rows(to // TILES), :],
            obuf.at[flip(source)],
            o_send.at[to], o_recv.at[source], device(plane, to),
        )

    def over_group(do):
        def body(t, carry):
            do((c + t) % CH)
            return carry

        lax.fori_loop(1, CH, body, 0)

    over_group(lambda to: adj_copy(to, c).start())

    table_copy = remote(
        tsend, tab.at[k, own_rows(s), :], t_send, t_recv.at[c], device(plane, LAST)
    )

    @pl.when(jnp.logical_not(last))
    def _():
        table_copy.start()

    for j in range(A):
        load(j, 2).wait()
    regroup(NF + 1, 2 * NF + 1)
    over_group(lambda to: frc_copy(to, c).start())

    ext[0, k, :, own_rows(s), :] = sbuf[chunk, 0:NF + 1]
    fa[k, :, own_rows(s), :] = sbuf[chunk, NF + 1:2 * NF + 1]

    for copy in small[3:]:
        copy.wait()
    high, low = split(inv[...])
    lhs[...] = jnp.concatenate([high, low, high], axis=1)

    xx32 = lanes((NR, 128)) % 32
    lane160 = lanes((ROWS, 128))
    xx160 = lane160 % 32
    lane40 = lanes((FOLD, 128))
    xx40 = lane40 % 32

    def plane_table(plane_to):
        return remote(
            tpl, tall.at[plane], u_send.at[plane_to], u_recv.at[plane],
            device(plane_to, LAST),
        )

    def plane_table_in(plane_from):
        return remote(
            tpl, tall.at[plane_from], u_send.at[plane_from], u_recv.at[plane_from],
            device(plane_from, LAST),
        )

    @pl.when(last)
    def _():
        tab[k, own_rows(s), :] = tsend[...]

        over_group(lambda source: remote(
            tsend, tab.at[source % TILES, own_rows(source // TILES), :],
            t_send, t_recv.at[source], device(plane, 0),
        ).wait_recv())
        merged = jnp.zeros((NR, 128), F32)
        for i in range(TILES):
            merged = jnp.where((xx32 == i) | (xx32 == 16 + i), tab[i], merged)
        tpl[...] = merged
        for d in range(1, PLANES):
            plane_table((plane + d) % PLANES).start()
        tall[plane] = merged
        for d in range(1, PLANES):
            plane_table_in((plane + d) % PLANES).wait_recv()
        column = jnp.zeros((NR, 128), F32)
        weight = jnp.zeros((NR, 128), F32)
        for i in range(PLANES):
            mine = xx32 // 8 == i
            column = jnp.where(mine, roll(tall[i], 8 * i), column)
            weight = jnp.where(mine, roll(tall[i], 8 * i - 16), weight)
        column = column - (plane * 32).astype(F32)
        here = (4 * (lanes((NR, 128)) % 8)).astype(F32)
        for shift in range(8):
            columns, weights = roll(column, -shift), roll(weight, -shift)
            for j in range(A):
                mtab[j, shift] = jnp.where(columns == here + j, weights, 0.0)
        for d in range(1, PLANES):
            plane_table((plane + d) % PLANES).wait_send()

    up = (plane + 1) % PLANES
    down = (plane + PLANES - 1) % PLANES
    nxt = unflip((chunk + 1) % CH)
    prv = unflip((chunk + CH - 1) % CH)

    def az_copy(n, side):
        return remote(
            hsend.at[n, side], hrecv.at[n, side], az_send.at[n, side], az_recv.at[n, side],
            device(up if side else down, c),
        )

    def ax_copy(n, side):
        if side == 0:
            return remote(psend.at[n, 0], hal.at[n, 1], ax_send.at[n, 0], ax_recv.at[n, 1], device(plane, prv))
        return remote(psend.at[n, 1], hal.at[n, 0], ax_send.at[n, 1], ax_recv.at[n, 0], device(plane, nxt))

    def ax_wait(n, side):
        return remote(psend.at[n, side], hal.at[n, side], ax_send.at[n, side], ax_recv.at[n, side], device(plane, nxt))

    def ex_copy(n, to):
        return remote(psend.at[n, 0], inl.at[n, plane], ex_send.at[n, to], ex_recv.at[n, plane], device(to, LAST))

    def ex_wait(n, source):
        return remote(psend.at[n, 0], inl.at[n, source], ex_send.at[n, source], ex_recv.at[n, source], device(source, 0))

    def field(n, kk):
        return ext[n, kk, 0:NF].reshape(ROWS, 128)

    half80 = lanes((ROWS // 2, 128)) < 64

    def send_az(n):
        for side in range(2):
            tile = field(n, side * (TILES - 1))
            near, far = tile[:ROWS // 2], roll(tile[ROWS // 2:], 64)
            hsend[n, side] = jnp.where(half80, far, near) if side else jnp.where(half80, near, far)
            az_copy(n, side).start()

    def halo(n, side):
        packed = hrecv[n, side]
        return jnp.concatenate([packed, roll(packed, 64)], axis=0)

    def send_ax(n):
        edges = [jnp.zeros((FOLD, 128), F32), jnp.zeros((FOLD, 128), F32)]
        for kk in range(TILES):
            tile = field(n, kk).reshape(NF, 4, R, 128)
            for q in range(4):
                rows = tile[:, q].reshape(FOLD, 128)
                to = 8 * q + kk
                edges[0] = jnp.where(xx40 == to, roll(rows, to), edges[0])
                edges[1] = jnp.where(xx40 == to, roll(rows, to - 31), edges[1])
        psend[n, 0] = edges[0]
        psend[n, 1] = edges[1]

        @pl.when(jnp.logical_not(first))
        def _():
            ax_copy(n, 0).start()

        @pl.when(jnp.logical_not(last))
        def _():
            ax_copy(n, 1).start()

        @pl.when(first)
        def _():
            for to in range(PLANES):
                ex_copy(n, to).start()

    def wait_adj(source):
        adj_copy(source, source).wait_recv()

    def wait_frc(source):
        frc_copy(source, source).wait_recv()

    over_group(wait_adj)
    send_az(0)
    send_ax(0)
    az = [[azc[f, g] * (1.0 / 12.0) for g in range(NF)] for f in range(NF)]
    ax = [[axc[f, g] * 0.5 for g in range(NF)] for f in range(NF)]

    def couple(coefficients, slope, f):
        total = coefficients[f][0] * slope[0:NR]
        for g in range(1, NF):
            total = total + coefficients[f][g] * slope[g * NR:(g + 1) * NR]
        return total

    def stencils(n, kk):
        here = field(n, kk)
        before = field(n, kk - 1) if kk else halo(n, 1)
        after = field(n, kk + 1) if kk < TILES - 1 else halo(n, 0)
        plus = roll(jnp.where(lane160 >= 32, here, after), 96)
        minus = roll(jnp.where(lane160 < 96, here, before), 32)
        far = roll(
            jnp.where(lane160 >= 64, here, after) - jnp.where(lane160 < 64, here, before), 64
        )
        slope = 8.0 * (plus - minus) - far
        along = jnp.where(xx160 == 31, 0.0, roll(here, 127)) - jnp.where(
            xx160 == 0, 0.0, roll(here, 1)
        )
        for f in range(NF):
            coupled = couple(az, slope, f) + couple(ax, along, f)
            right = here[f * NR:(f + 1) * NR] - ext[0, kk, NF] * coupled
            rhs[kk, f] = right.reshape(4, R, 128)

    def couple_edges(n):
        sides = []
        for side, sign in ((0, -1.0), (1, 1.0)):
            edge = hal[n, side].reshape(NF, R, 128)
            rows = []
            for f in range(NF):
                total = ax[f][0] * edge[0]
                for g in range(1, NF):
                    total = total + ax[f][g] * edge[g]
                rows.append(sign * total)
            sides.append(jnp.concatenate(rows, axis=0))
        return sides

    def with_edges(kk, edges):
        right = rhs[kk]
        groups = []
        for q in range(4):
            at = 8 * q + kk
            edge = jnp.where(
                xx40 == 31, roll(edges[1], 31 - at), jnp.where(xx40 == 0, roll(edges[0], -at), 0.0)
            ).reshape(NF, R, 128)
            scale = ext[0, kk, NF, q * R:(q + 1) * R]
            groups.append(
                right[:, q] + fa[kk, :, q * R:(q + 1) * R] - scale[None] * edge
            )
        return jnp.stack(groups, axis=1).reshape(ROWS, 128)

    def exit_plane(n):
        for source in range(PLANES):
            ex_wait(n, source).wait_recv()
        for q in range(4):
            inlet = jnp.zeros((FOLD, 128), F32)
            for i in range(PLANES):
                inlet = jnp.where(xx40 // 8 == i, roll(inl[n, i], 8 * (i - q)), inlet)
            sums = [None] * A
            for shift in range(8):
                moved = roll(inlet, -shift)
                for j in range(A):
                    tile = mtab[j, shift, q * R:(q + 1) * R]
                    term = moved * jnp.concatenate([tile] * NF, axis=0)
                    sums[j] = term if sums[j] is None else sums[j] + term
            odd = (lane40 // 32) % 2 == 1
            pairs = [
                jnp.where(odd, sums[j + 1], sums[j]) + roll(jnp.where(odd, sums[j], sums[j + 1]), -32)
                for j in (0, 2)
            ]
            upper = lane40 >= 64
            total = jnp.where(upper, pairs[1], pairs[0]) + roll(
                jnp.where(upper, pairs[0], pairs[1]), -64
            )
            total = total + roll(total, -8)
            total = total + roll(total, -16)
            for kk in range(TILES):
                placed = jnp.where(xx40 == 31, roll(total, 31 - kk), 0.0)
                rhs[kk, :, q] += placed.reshape(NF, R, 128)

    def solve(n, pair, edges):
        high, low = split(jnp.concatenate(
            [with_edges(2 * pair + i, edges) for i in range(2)], axis=1
        ))
        solved = jnp.dot(lhs[...], jnp.concatenate([high, high, low], axis=0), preferred_element_type=F32)
        for i in range(2):
            ext[n + 1, 2 * pair + i, 0:NF] = solved[:, i * 128:(i + 1) * 128].reshape(NF, NR, 128)

    def sweep(n, carry):
        for kk in range(1, TILES - 1):
            stencils(n, kk)
        for side in range(2):
            az_copy(n, side).wait_recv()
        stencils(n, 0)
        stencils(n, TILES - 1)

        @pl.when(jnp.logical_not(first))
        def _():
            ax_wait(n, 0).wait_recv()

        @pl.when(jnp.logical_not(last))
        def _():
            ax_wait(n, 1).wait_recv()

        @pl.when(n == 0)
        def _():
            over_group(wait_frc)

        edges = couple_edges(n)

        @pl.when(last)
        def _():
            exit_plane(n)

        solve(n, 0, edges)
        solve(n, 3, edges)

        @pl.when(n < ITERS - 1)
        def _():
            send_az(n + 1)

        solve(n, 1, edges)
        solve(n, 2, edges)

        @pl.when(n < ITERS - 1)
        def _():
            send_ax(n + 1)

        return carry

    lax.fori_loop(0, ITERS, sweep, 0)

    over_group(lambda to: out_copy(to, c).start())
    obuf[chunk] = ext[ITERS, k, 0:NF, own_rows(s), :]

    def back(step, carry):
        t = (chunk // A + CH // A - step) % (CH // A)
        for i in range(A):
            source = unflip(t * A + i)

            @pl.when(source != c)
            def _():
                out_copy(source, source).wait_recv()

        at = pl.ds(pl.multiple_of(t * 128, 128), 128)
        for f in range(NF):
            pieces = swap_groups([obuf[t * A + i, f] for i in range(A)], lane8)
            for j in range(A):
                out[f, :, j, at] = pieces[j]
        return carry

    lax.fori_loop(1, CH // A + 1, back, 0)

    def sent(to):
        adj_copy(to, c).wait_send()
        frc_copy(to, c).wait_send()
        out_copy(to, c).wait_send()

    over_group(sent)

    @pl.when(jnp.logical_not(last))
    def _():
        table_copy.wait_send()

    def sweep_sent(n, carry):
        for side in range(2):
            az_copy(n, side).wait_send()

        @pl.when(jnp.logical_not(first))
        def _():
            ax_copy(n, 0).wait_send()

        @pl.when(jnp.logical_not(last))
        def _():
            ax_copy(n, 1).wait_send()

        @pl.when(first)
        def _():
            for to in range(PLANES):
                ex_copy(n, to).wait_send()

        return carry

    lax.fori_loop(0, ITERS, sweep_sent, 0)


def per_device(
    adjoint, forcing, area_scale, azimuth_coupling, axial_coupling,
    inverse, owner_device, owner_slot, weight,
):
    vmem = pl.BlockSpec(memory_space=pltpu.VMEM)
    hbm = pl.BlockSpec(memory_space=pltpu.HBM)
    dma = pltpu.SemaphoreType.DMA
    return pl.pallas_call(
        kernel,
        out_shape=jax.ShapeDtypeStruct(adjoint.shape, F32),
        in_specs=[hbm] * 9,
        out_specs=vmem,
        scratch_shapes=[
            pltpu.VMEM((2 * NF + 1, A, R, CH * 32), F32),
            dma((3, A)),
            pltpu.SMEM((NF, NF), F32),
            pltpu.SMEM((NF, NF), F32),
            pltpu.VMEM((ROWS, ROWS), F32),
            pltpu.VMEM((A, 1, R), jnp.int32),
            pltpu.VMEM((A, 1, R), jnp.int32),
            pltpu.VMEM((A, 1, R), F32),
            dma((6,)),
            pltpu.VMEM((R, 128), F32),
            pltpu.VMEM((ITERS, 2, ROWS // 2, 128), F32),
            pltpu.VMEM((ITERS, 2, ROWS // 2, 128), F32),
            pltpu.VMEM((CH, 2 * NF + 1, R, 128), F32),
            pltpu.VMEM((ITERS + 1, TILES, NF + 1, NR, 128), F32),
            pltpu.VMEM((TILES, NF, NR, 128), F32),
            pltpu.VMEM((ITERS, 2, FOLD, 128), F32),
            pltpu.VMEM((ITERS, 2, FOLD, 128), F32),
            pltpu.VMEM((ITERS, PLANES, FOLD, 128), F32),
            pltpu.VMEM((CH, NF, R, 128), F32),
            pltpu.VMEM((TILES, NR, 128), F32),
            pltpu.VMEM((NR, 128), F32),
            pltpu.VMEM((PLANES, NR, 128), F32),
            pltpu.VMEM((A, 8, NR, 128), F32),
            pltpu.VMEM((ROWS, 3 * ROWS), BF16),
            pltpu.VMEM((TILES, NF, 4, R, 128), F32),
            dma((CH,)), dma((CH,)), dma((CH,)), dma((CH,)), dma((CH,)), dma((CH,)),
            dma((ITERS, 2)), dma((ITERS, 2)), dma((ITERS, 2)), dma((ITERS, 2)),
            dma((ITERS, PLANES)), dma((ITERS, PLANES)),
            dma(()), dma((CH,)), dma((PLANES,)), dma((PLANES,)),
        ],
        compiler_params=pltpu.CompilerParams(
            collective_id=0, has_side_effects=True, vmem_limit_bytes=60 * 1024 * 1024
        ),
    )(
        adjoint, forcing, area_scale, azimuth_coupling, axial_coupling, inverse,
        owner_device.reshape(A, 1, R), owner_slot.reshape(A, 1, R), weight.reshape(A, 1, R),
    )


def solution(mesh):
    return jax.shard_map(
        per_device,
        mesh=mesh,
        in_specs=(
            P(None, "span", "passage", None),
            P(None, "span", "passage", None),
            P(None, "span", "passage", None),
            P(),
            P(),
            P("span", None, None),
            P("span", "passage", None, None),
            P("span", "passage", None, None),
            P("span", "passage", None, None),
        ),
        out_specs=P(None, "span", "passage", None),
        check_vma=False,
    )
```

```python
import jax
import jax.numpy as jnp
from jax import lax
from jax.experimental import pallas as pl
from jax.experimental.pallas import tpu as pltpu
from jax.sharding import PartitionSpec as P

ITERS = 4
MESH = pl.DeviceIdType.MESH
NF = 5
R = 8
NR = 32
ROWS = NF * NR
A = 4
CH = 32
TILES = 8
PLANES = 4
FOLD = 40
F32 = jnp.float32
BF16 = jnp.bfloat16


def flip(member):
    span, k = member // TILES, member % TILES
    at = k + k // 4 * (11 - 2 * k)
    return span * TILES + at + span % 2 * (7 - 2 * at)


def unflip(chunk):
    span, at = chunk // TILES, chunk % TILES
    at = at + span % 2 * (7 - 2 * at)
    return span * TILES + at + at // 4 * (11 - 2 * at)


LAST = unflip(CH - 1)


def lanes(shape):
    return lax.broadcasted_iota(jnp.int32, shape, len(shape) - 1)


def roll(x, by):
    by = by % 128
    return x if by == 0 else pltpu.roll(x, by, x.ndim - 1)


def swap_groups(v, lane):
    half = lane < 64
    odd = (lane // 32) % 2 == 1
    c0 = jnp.where(half, v[0], roll(v[2], 64))
    c2 = jnp.where(half, roll(v[0], 64), v[2])
    c1 = jnp.where(half, v[1], roll(v[3], 64))
    c3 = jnp.where(half, roll(v[1], 64), v[3])
    return [
        jnp.where(odd, roll(c1, 32), c0),
        jnp.where(odd, c1, roll(c0, 96)),
        jnp.where(odd, roll(c3, 32), c2),
        jnp.where(odd, c3, roll(c2, 96)),
    ]


def split(x):
    high = x.astype(BF16)
    return high, (x - high.astype(F32)).astype(BF16)


def kernel(
    adj, frc, area, azc_in, axc_in, inv_in, owner, slot_in, weight_in, out,
    xin, in_sem, azc, axc, inv, owner_at, slot_at, weight_at, small_sem, tsend, hsend, hrecv, sbuf, ext, fa, psend, hal, inl, obuf, tab, tpl, tall, mtab, lhs, rhs, edgeb, areap,
    a_send, a_recv, f_send, f_recv, o_send, o_recv,
    az_send, az_recv, ax_send, ax_recv, ex_send, ex_recv,
    t_send, t_recv, u_send, u_recv,
):
    p = lax.axis_index("passage")
    s = lax.axis_index("span")
    plane = p // TILES
    k = p % TILES
    c = s * TILES + k
    chunk = flip(c)
    first = chunk == 0
    last = chunk == CH - 1

    def device(plane_at, chunk):
        return (plane_at * TILES + chunk % TILES, chunk // TILES)

    def remote(src, dst, send, recv, to):
        return pltpu.make_async_remote_copy(
            src_ref=src, dst_ref=dst, send_sem=send, recv_sem=recv,
            device_id=to, device_id_type=MESH,
        )

    def own_rows(span):
        return pl.ds(pl.multiple_of(span * R, R), R)

    def load(j, which):
        src, at, count = ((adj, 0, NF), (area, NF, 1), (frc, NF + 1, NF))[which]
        return pltpu.make_async_copy(
            src.at[:, :, j, :], xin.at[pl.ds(at, count), j], in_sem.at[which, j]
        )

    small = [
        pltpu.make_async_copy(source, to, small_sem.at[i])
        for i, (source, to) in enumerate((
            (owner, owner_at), (slot_in, slot_at), (weight_in, weight_at),
            (azc_in, azc), (axc_in, axc), (inv_in.at[chunk % TILES // (TILES // 2)], inv),
        ))
    ]
    for j in range(A):
        load(j, 0).start()
    for copy in small:
        copy.start()
    for which in range(1, 3):
        for j in range(A):
            load(j, which).start()

    barrier = pltpu.get_barrier_semaphore()

    def greet(plane_at, chunk):
        pl.semaphore_signal(barrier, inc=1, device_id=device(plane_at, chunk), device_id_type=MESH)

    def greet_group(t, carry):
        greet(plane, (c + t) % CH)
        return carry

    lax.fori_loop(1, CH, greet_group, 0)
    for d in range(1, PLANES):
        greet((plane + d) % PLANES, c)

    @pl.when(first)
    def _():
        for d in range(1, PLANES):
            greet((plane + d) % PLANES, LAST)

    @pl.when(last)
    def _():
        for d in range(1, PLANES):
            greet((plane + d) % PLANES, 0)

    lane8 = lanes((R, 128))

    def regroup(low, high):
        def body(t, carry):
            at = pl.ds(pl.multiple_of(t * 128, 128), 128)
            for slot in range(low, high):
                pieces = swap_groups([xin[slot, j, :, at] for j in range(A)], lane8)
                for i in range(A):
                    sbuf[t * A + i, slot] = pieces[i]
            return carry

        lax.fori_loop(0, CH // A, body, 0)

    for copy in small[:3]:
        copy.wait()
    diagonal = lax.broadcasted_iota(jnp.int32, (R, R), 0) == lanes((R, R))
    tables = [jnp.zeros((R, 128), F32)] * 2
    for j in range(A):
        column = (owner_at[j] * A + slot_at[j]).astype(F32)
        for i, row in enumerate((column, weight_at[j])):
            upright = jnp.sum(jnp.where(diagonal, row, 0.0), axis=1, keepdims=True)
            tables[i] = jnp.where(lane8 // 32 == j, upright, tables[i])
    for i in range(2):
        tsend[i] = tables[i]

    for which in range(2):
        for j in range(A):
            load(j, which).wait()
    regroup(0, NF + 1)
    hal[...] = jnp.zeros_like(hal)

    edge = jnp.logical_or(first, last)
    peers = CH - 1 + PLANES - 1

    @pl.when(edge)
    def _():
        pl.semaphore_wait(barrier, peers + PLANES - 1)

    @pl.when(jnp.logical_not(edge))
    def _():
        pl.semaphore_wait(barrier, peers)

    def adj_copy(to, source):
        return remote(
            sbuf.at[flip(to), pl.ds(0, NF + 1)],
            ext.at[0, source % TILES, :, own_rows(source // TILES), :],
            a_send.at[to], a_recv.at[source], device(plane, to),
        )

    def frc_copy(to, source):
        return remote(
            sbuf.at[flip(to), pl.ds(NF + 1, NF)],
            fa.at[source % TILES, :, own_rows(source // TILES), :],
            f_send.at[to], f_recv.at[source], device(plane, to),
        )

    def out_copy(to, source):
        return remote(
            ext.at[ITERS, to % TILES, pl.ds(0, NF), own_rows(to // TILES), :],
            obuf.at[flip(source)],
            o_send.at[to], o_recv.at[source], device(plane, to),
        )

    def over_group(do):
        def body(t, carry):
            do((c + t) % CH)
            return carry

        lax.fori_loop(1, CH, body, 0)

    over_group(lambda to: adj_copy(to, c).start())

    table_copy = remote(
        tsend, tab.at[k, :, own_rows(s), :], t_send, t_recv.at[c], device(plane, LAST)
    )

    @pl.when(jnp.logical_not(last))
    def _():
        table_copy.start()

    for j in range(A):
        load(j, 2).wait()
    regroup(NF + 1, 2 * NF + 1)
    over_group(lambda to: frc_copy(to, c).start())

    ext[0, k, :, own_rows(s), :] = sbuf[chunk, 0:NF + 1]
    fa[k, :, own_rows(s), :] = sbuf[chunk, NF + 1:2 * NF + 1]

    for copy in small[3:]:
        copy.wait()
    high, low = split(inv[...])
    lhs[...] = jnp.concatenate([high, low, high], axis=1)

    xx32 = lanes((NR, 128)) % 32
    lane160 = lanes((ROWS, 128))
    xx160 = lane160 % 32
    lane40 = lanes((FOLD, 128))
    xx40 = lane40 % 32

    def plane_table(plane_to):
        return remote(
            tpl, tall.at[plane], u_send.at[plane_to], u_recv.at[plane],
            device(plane_to, LAST),
        )

    def plane_table_in(plane_from):
        return remote(
            tpl, tall.at[plane_from], u_send.at[plane_from], u_recv.at[plane_from],
            device(plane_from, LAST),
        )

    @pl.when(last)
    def _():
        tab[k, :, own_rows(s), :] = tsend[...]

        over_group(lambda source: remote(
            tsend, tab.at[source % TILES, :, own_rows(source // TILES), :],
            t_send, t_recv.at[source], device(plane, 0),
        ).wait_recv())
        for which in range(2):
            merged = tab[0, which]
            for i in range(1, TILES):
                merged = jnp.where(xx32 // 4 == i, tab[i, which], merged)
            tpl[which] = merged
        for d in range(1, PLANES):
            plane_table((plane + d) % PLANES).start()
        tall[plane] = tpl[...]
        for d in range(1, PLANES):
            plane_table_in((plane + d) % PLANES).wait_recv()
        column, weight = tall[0, 0], tall[0, 1]
        for i in range(1, PLANES):
            mine = xx32 % 4 == i
            column = jnp.where(mine, tall[i, 0], column)
            weight = jnp.where(mine, tall[i, 1], weight)
        column = column - (plane * 32).astype(F32)
        here = (4 * (xx32 // 4)).astype(F32)
        for shift in range(8):
            columns, weights = roll(column, -4 * shift), roll(weight, -4 * shift)
            for j in range(A):
                mtab[j, shift] = jnp.where(columns == here + j, weights, 0.0)
        for d in range(1, PLANES):
            plane_table((plane + d) % PLANES).wait_send()

    up = (plane + 1) % PLANES
    down = (plane + PLANES - 1) % PLANES
    nxt = unflip((chunk + 1) % CH)
    prv = unflip((chunk + CH - 1) % CH)

    def az_copy(n, side):
        return remote(
            hsend.at[n, side], hrecv.at[n, side], az_send.at[n, side], az_recv.at[n, side],
            device(up if side else down, c),
        )

    def ax_copy(n, side):
        if side == 0:
            return remote(psend.at[n, 0], hal.at[n, 1], ax_send.at[n, 0], ax_recv.at[n, 1], device(plane, prv))
        return remote(psend.at[n, 1], hal.at[n, 0], ax_send.at[n, 1], ax_recv.at[n, 0], device(plane, nxt))

    def ax_wait(n, side):
        return remote(psend.at[n, side], hal.at[n, side], ax_send.at[n, side], ax_recv.at[n, side], device(plane, nxt))

    def ex_copy(n, to):
        return remote(psend.at[n, 0], inl.at[n, plane], ex_send.at[n, to], ex_recv.at[n, plane], device(to, LAST))

    def ex_wait(n, source):
        return remote(psend.at[n, 0], inl.at[n, source], ex_send.at[n, source], ex_recv.at[n, source], device(source, 0))

    def field(n, kk):
        return ext[n, kk, 0:NF].reshape(ROWS, 128)

    half80 = lanes((ROWS // 2, 128)) < 64

    def send_az(n):
        for side in range(2):
            tile = field(n, side * (TILES - 1))
            near, far = tile[:ROWS // 2], roll(tile[ROWS // 2:], 64)
            hsend[n, side] = jnp.where(half80, far, near) if side else jnp.where(half80, near, far)
            az_copy(n, side).start()

    def halo(n, side):
        packed = hrecv[n, side]
        return jnp.concatenate([packed, roll(packed, 64)], axis=0)

    def send_ax(n):
        edges = [jnp.zeros((FOLD, 128), F32), jnp.zeros((FOLD, 128), F32)]
        for kk in range(TILES):
            tile = field(n, kk).reshape(NF, 4, R, 128)
            for q in range(4):
                rows = tile[:, q].reshape(FOLD, 128)
                to = 4 * kk + q
                moved = roll(rows, to)
                edges[0] = jnp.where(xx40 == to, moved, edges[0])
                edges[1] = jnp.where(xx40 == (to + 31) % 32, moved, edges[1])
        psend[n, 0] = edges[0]
        psend[n, 1] = edges[1]

        @pl.when(jnp.logical_not(first))
        def _():
            ax_copy(n, 0).start()

        @pl.when(jnp.logical_not(last))
        def _():
            ax_copy(n, 1).start()

        @pl.when(first)
        def _():
            for to in range(PLANES):
                ex_copy(n, to).start()

    def wait_adj(source):
        adj_copy(source, source).wait_recv()

    def wait_frc(source):
        frc_copy(source, source).wait_recv()

    over_group(wait_adj)
    send_az(0)
    send_ax(0)
    scales = [jnp.zeros((R, 128), F32)] * 2
    for kk in range(TILES):
        for q in range(4):
            rows = ext[0, kk, NF, q * R:(q + 1) * R]
            to = 4 * kk + q
            scales[0] = jnp.where(lane8 % 32 == (to + 31) % 32, roll(rows, to + 31), scales[0])
            scales[1] = jnp.where(lane8 % 32 == to, roll(rows, to - 31), scales[1])
    for side in range(2):
        areap[side] = scales[side]

    az = [[azc[f, g] * (1.0 / 12.0) for g in range(NF)] for f in range(NF)]
    ax = [[axc[f, g] * 0.5 for g in range(NF)] for f in range(NF)]

    def couple(coefficients, slope, f):
        total = coefficients[f][0] * slope[0:NR]
        for g in range(1, NF):
            total = total + coefficients[f][g] * slope[g * NR:(g + 1) * NR]
        return total

    def stencils(n, kk):
        here = field(n, kk)
        before = field(n, kk - 1) if kk else halo(n, 1)
        after = field(n, kk + 1) if kk < TILES - 1 else halo(n, 0)
        plus = roll(jnp.where(lane160 >= 32, here, after), 96)
        minus = roll(jnp.where(lane160 < 96, here, before), 32)
        far = roll(
            jnp.where(lane160 >= 64, here, after) - jnp.where(lane160 < 64, here, before), 64
        )
        slope = 8.0 * (plus - minus) - far
        along = jnp.where(xx160 == 31, 0.0, roll(here, 127)) - jnp.where(
            xx160 == 0, 0.0, roll(here, 1)
        )
        for f in range(NF):
            coupled = couple(az, slope, f) + couple(ax, along, f)
            right = here[f * NR:(f + 1) * NR] - ext[0, kk, NF] * coupled
            rhs[kk, f] = right.reshape(4, R, 128)

    def couple_edges(n):
        sides = []
        for side, sign in ((0, -1.0), (1, 1.0)):
            edge = hal[n, side].reshape(NF, R, 128)
            rows = []
            for f in range(NF):
                total = ax[f][0] * edge[0]
                for g in range(1, NF):
                    total = total + ax[f][g] * edge[g]
                rows.append(sign * total)
            sides.append(jnp.concatenate(rows, axis=0))
        return sides

    def place_edges(n):
        sides = couple_edges(n)
        for side in range(2):
            sides[side] = -jnp.concatenate([areap[side]] * NF, axis=0) * sides[side]
        for q in range(4):
            edge = jnp.where(
                xx40 % 4 == 1, roll(sides[0], -30 - q),
                jnp.where(xx40 % 4 == 0, roll(sides[1], 32 - q), 0.0),
            )
            edgeb[:, q] = edge.reshape(NF, R, 128)

    def times_inverse(right):
        high, low = split(right)
        return jnp.dot(
            lhs[...], jnp.concatenate([high, high, low], axis=0), preferred_element_type=F32
        )

    def add_edges(n, solved, kk):
        moved = roll(solved, -(4 * kk + 1))
        edge = jnp.where((xx160 == 0) | (xx160 == 31), moved, 0.0)
        ext[n + 1, kk, 0:NF] += edge.reshape(NF, NR, 128)

    def exit_plane(n):
        for source in range(PLANES):
            ex_wait(n, source).wait_recv()
        for q in range(4):
            inlet = jnp.zeros((FOLD, 128), F32)
            for i in range(PLANES):
                inlet = jnp.where(xx40 % 4 == i, roll(inl[n, i], i - q), inlet)
            sums = [None] * A
            for shift in range(8):
                moved = roll(inlet, -4 * shift)
                for j in range(A):
                    tile = mtab[j, shift, q * R:(q + 1) * R]
                    term = moved * jnp.concatenate([tile] * NF, axis=0)
                    sums[j] = term if sums[j] is None else sums[j] + term
            odd = (lane40 // 32) % 2 == 1
            pairs = [
                jnp.where(odd, sums[j + 1], sums[j]) + roll(jnp.where(odd, sums[j], sums[j + 1]), -32)
                for j in (0, 2)
            ]
            upper = lane40 >= 64
            total = jnp.where(upper, pairs[1], pairs[0]) + roll(
                jnp.where(upper, pairs[0], pairs[1]), -64
            )
            total = total + roll(total, -1)
            total = total + roll(total, -2)
            edgeb[:, q] += jnp.where(xx40 % 4 == 0, roll(total, 32), 0.0).reshape(NF, R, 128)

    def solve(n, pair):
        tiles = [2 * pair + i for i in range(2)]
        solved = times_inverse(jnp.concatenate(
            [rhs[kk].reshape(ROWS, 128) + fa[kk].reshape(ROWS, 128) for kk in tiles], axis=1
        ))
        for i in range(2):
            ext[n + 1, 2 * pair + i, 0:NF] = solved[:, i * 128:(i + 1) * 128].reshape(NF, NR, 128)

    def received_edges(n):
        @pl.when(jnp.logical_not(first))
        def _():
            ax_wait(n, 0).wait_recv()

        @pl.when(jnp.logical_not(last))
        def _():
            ax_wait(n, 1).wait_recv()

        place_edges(n)

        @pl.when(last)
        def _():
            exit_plane(n)

        return times_inverse(edgeb[...].reshape(ROWS, 128))

    def first_sweep(n):
        for kk in range(1, TILES - 1):
            stencils(n, kk)
        for side in range(2):
            az_copy(n, side).wait_recv()
        stencils(n, 0)
        stencils(n, TILES - 1)
        solved = received_edges(n)
        over_group(wait_frc)
        solve(n, 0)
        add_edges(n, solved, 0)
        solve(n, 3)
        add_edges(n, solved, TILES - 1)
        send_az(n + 1)
        add_edges(n, solved, 1)
        add_edges(n, solved, TILES - 2)
        for pair in (1, 2):
            solve(n, pair)
            add_edges(n, solved, 2 * pair)
            add_edges(n, solved, 2 * pair + 1)
        send_ax(n + 1)

    def sweep(n, carry):
        for kk in range(1, TILES - 1):
            stencils(n, kk)
        solve(n, 1)
        solve(n, 2)
        for side in range(2):
            az_copy(n, side).wait_recv()
        stencils(n, 0)
        stencils(n, TILES - 1)
        solve(n, 0)
        solve(n, 3)

        solved = received_edges(n)
        add_edges(n, solved, 0)
        add_edges(n, solved, TILES - 1)

        @pl.when(n < ITERS - 1)
        def _():
            send_az(n + 1)

        for kk in range(1, TILES - 1):
            add_edges(n, solved, kk)

        @pl.when(n < ITERS - 1)
        def _():
            send_ax(n + 1)

        return carry

    first_sweep(0)
    lax.fori_loop(1, ITERS, sweep, 0)

    over_group(lambda to: out_copy(to, c).start())
    obuf[chunk] = ext[ITERS, k, 0:NF, own_rows(s), :]

    def back(step, carry):
        t = (chunk // A + CH // A - step) % (CH // A)
        for i in range(A):
            source = unflip(t * A + i)

            @pl.when(source != c)
            def _():
                out_copy(source, source).wait_recv()

        at = pl.ds(pl.multiple_of(t * 128, 128), 128)
        for f in range(NF):
            pieces = swap_groups([obuf[t * A + i, f] for i in range(A)], lane8)
            for j in range(A):
                out[f, :, j, at] = pieces[j]
        return carry

    lax.fori_loop(1, CH // A + 1, back, 0)

    def sent(to):
        adj_copy(to, c).wait_send()
        frc_copy(to, c).wait_send()
        out_copy(to, c).wait_send()

    over_group(sent)

    @pl.when(jnp.logical_not(last))
    def _():
        table_copy.wait_send()

    def sweep_sent(n, carry):
        for side in range(2):
            az_copy(n, side).wait_send()

        @pl.when(jnp.logical_not(first))
        def _():
            ax_copy(n, 0).wait_send()

        @pl.when(jnp.logical_not(last))
        def _():
            ax_copy(n, 1).wait_send()

        @pl.when(first)
        def _():
            for to in range(PLANES):
                ex_copy(n, to).wait_send()

        return carry

    lax.fori_loop(0, ITERS, sweep_sent, 0)


def per_device(
    adjoint, forcing, area_scale, azimuth_coupling, axial_coupling,
    inverse, owner_device, owner_slot, weight,
):
    vmem = pl.BlockSpec(memory_space=pltpu.VMEM)
    hbm = pl.BlockSpec(memory_space=pltpu.HBM)
    dma = pltpu.SemaphoreType.DMA
    return pl.pallas_call(
        kernel,
        out_shape=jax.ShapeDtypeStruct(adjoint.shape, F32),
        in_specs=[hbm] * 9,
        out_specs=vmem,
        scratch_shapes=[
            pltpu.VMEM((2 * NF + 1, A, R, CH * 32), F32),
            dma((3, A)),
            pltpu.SMEM((NF, NF), F32),
            pltpu.SMEM((NF, NF), F32),
            pltpu.VMEM((ROWS, ROWS), F32),
            pltpu.VMEM((A, 1, R), jnp.int32),
            pltpu.VMEM((A, 1, R), jnp.int32),
            pltpu.VMEM((A, 1, R), F32),
            dma((6,)),
            pltpu.VMEM((2, R, 128), F32),
            pltpu.VMEM((ITERS, 2, ROWS // 2, 128), F32),
            pltpu.VMEM((ITERS, 2, ROWS // 2, 128), F32),
            pltpu.VMEM((CH, 2 * NF + 1, R, 128), F32),
            pltpu.VMEM((ITERS + 1, TILES, NF + 1, NR, 128), F32),
            pltpu.VMEM((TILES, NF, NR, 128), F32),
            pltpu.VMEM((ITERS, 2, FOLD, 128), F32),
            pltpu.VMEM((ITERS, 2, FOLD, 128), F32),
            pltpu.VMEM((ITERS, PLANES, FOLD, 128), F32),
            pltpu.VMEM((CH, NF, R, 128), F32),
            pltpu.VMEM((TILES, 2, NR, 128), F32),
            pltpu.VMEM((2, NR, 128), F32),
            pltpu.VMEM((PLANES, 2, NR, 128), F32),
            pltpu.VMEM((A, 8, NR, 128), F32),
            pltpu.VMEM((ROWS, 3 * ROWS), BF16),
            pltpu.VMEM((TILES, NF, 4, R, 128), F32),
            pltpu.VMEM((NF, 4, R, 128), F32),
            pltpu.VMEM((2, R, 128), F32),
            dma((CH,)), dma((CH,)), dma((CH,)), dma((CH,)), dma((CH,)), dma((CH,)),
            dma((ITERS, 2)), dma((ITERS, 2)), dma((ITERS, 2)), dma((ITERS, 2)),
            dma((ITERS, PLANES)), dma((ITERS, PLANES)),
            dma(()), dma((CH,)), dma((PLANES,)), dma((PLANES,)),
        ],
        compiler_params=pltpu.CompilerParams(
            collective_id=0, has_side_effects=True, vmem_limit_bytes=60 * 1024 * 1024
        ),
    )(
        adjoint, forcing, area_scale, azimuth_coupling, axial_coupling, inverse,
        owner_device.reshape(A, 1, R), owner_slot.reshape(A, 1, R), weight.reshape(A, 1, R),
    )


def solution(mesh):
    return jax.shard_map(
        per_device,
        mesh=mesh,
        in_specs=(
            P(None, "span", "passage", None),
            P(None, "span", "passage", None),
            P(None, "span", "passage", None),
            P(),
            P(),
            P("span", None, None),
            P("span", "passage", None, None),
            P("span", "passage", None, None),
            P("span", "passage", None, None),
        ),
        out_specs=P(None, "span", "passage", None),
        check_vma=False,
    )
```
